128 devices in a mesh: seq: 32 (over z, x, core), kvh: 4 (over y).
Axes of the slice: x: 4, y: 4, z: 4, core: 2. Of those that a mesh axis runs over, the one named last changes fastest.
Arguments:
- queries: bfloat16 [8192, 32, 128], P('seq', 'kvh'), may hold values from -6 to 6
- ctx_keys: bfloat16 [131072, 8, 128], P('seq', 'kvh'), may hold values from -6 to 6
- ctx_values: bfloat16 [131072, 8, 128], P('seq', 'kvh'), may hold values from -6 to 6
- new_keys: bfloat16 [8192, 8, 128], P('seq', 'kvh'), may hold values from -6 to 6
- new_values: bfloat16 [8192, 8, 128], P('seq', 'kvh'), may hold values from -6 to 6
- picks: int32 [8, 512, 2], P('kvh', 'seq'), may hold values from 0 to 31, all different within a row; in each aligned block of 16 rows (0 to 15, 16 to 31, ..., all dimensions but the last counted through in order) at most 2 rows name the same one
- out_weight: bfloat16 [4096, 4096], P('kvh'), may hold values from -0.09375 to 0.09375
Outputs:
- projected: bfloat16 [8192, 4096], P(('seq', 'kvh'))
The draws below stay inside these ranges and needn't reach their ends.
Inputs may be any that keep to these rules, and one draw needn't show every extreme that they name: In each aligned block of 16 rows of picks (one key-value head's query blocks on one index of seq) the 2 entries of a row differ and no context block is named more than 2 times; some block is named exactly 2 times.
All inputs are finite; a program needn't handle non-finite values.
Results may differ from the reference program's by a relative error of at most 0.015.
Values may be sent and summed in bfloat16 or wider, within the bound.
A program may use at most 256 MiB of HBM per device.

```python
import math
import jax
import jax.numpy as jnp
import numpy as np
from jax import lax

HQ = 32
KVH = 8
D_HEAD = 128
DM = 4096
KB = 4096
QB = 16
PICKS = 2
QB_DEV = 16
STRETCH = 8192
NQB = 512
NCTX = 32
CTX = 131072
CAP = 2


def draw_queries(key, part):
    key = jax.random.fold_in(key, 11)
    base = jax.random.normal(key, (STRETCH, HQ, D_HEAD), jnp.float32)
    return jnp.clip(base, -6.0, 6.0).astype(jnp.bfloat16)


def draw_ctx_keys(key, part):
    key = jax.random.fold_in(key, 12)
    base = jax.random.normal(key, (CTX, KVH, D_HEAD), jnp.float32)
    return jnp.clip(base, -6.0, 6.0).astype(jnp.bfloat16)


def draw_new_keys(key, part):
    key = jax.random.fold_in(key, 13)
    base = jax.random.normal(key, (STRETCH, KVH, D_HEAD), jnp.float32)
    return jnp.clip(base, -6.0, 6.0).astype(jnp.bfloat16)


def block_scale(own_key, extent, split, smallest, largest):
    level = 1.0
    for position, blocks in split:
        steps = jax.random.uniform(jax.random.fold_in(jax.random.fold_in(own_key, 6), position), (blocks,), jnp.float32, smallest / len(split), largest / len(split))
        level = level * jnp.repeat(jnp.exp(steps), extent[position] // blocks).reshape((-1,) + (1,) * (len(extent) - 1 - position))
    return level


def shared_out(stream_key, own, number, rows, count, top, most, skew):
    ranking = jax.random.permutation(stream_key, count)
    heavy_load, ordinary = portions_of(count, rows * top, most, skew, True), portions_of(count, rows * top, most, skew, False)
    places = jnp.arange(count)

    def named(tallies, rotation):
        used = int((tallies > 0).sum())
        fixed = max(1, used // 4)
        passed = fixed + (places - fixed + rotation * (used - fixed)) % max(1, count - fixed)
        return jnp.zeros((count,), jnp.int32).at[ranking[jnp.where(places < fixed, places, passed)]].set(jnp.asarray(tallies, jnp.int32))

    tallies = jnp.where(number % 4 == 0, named(heavy_load, number // 4), named(ordinary, number - number // 4 - 1))
    mixed = jax.random.permutation(jax.random.fold_in(own, 3), count)
    giver, sink = mixed[0:count // 2 * 2:2], mixed[1:count // 2 * 2:2]
    room = jnp.minimum(tallies[giver] - 1, most - tallies[sink]) // 2
    room = jnp.where((giver == ranking[0]) | (sink == ranking[0]) | (tallies[sink] == 0), 0, jnp.maximum(room, 0))
    passed = jax.random.randint(jax.random.fold_in(own, 4), (count // 2,), 0, 1 << 20) % (room + 1)
    tallies = tallies.at[giver].add(-passed).at[sink].add(passed)
    items = jnp.searchsorted(jnp.cumsum(tallies), jnp.arange(rows * top), side="right").astype(jnp.int32)
    table = items.reshape(top, rows).T
    table = table[jax.random.permutation(jax.random.fold_in(own, 1), rows)]
    rotation = jax.random.randint(jax.random.fold_in(own, 2), (rows, 1), 0, top)
    return jnp.take_along_axis(table, (jnp.arange(top)[None, :] + rotation) % top, axis=1)


def portions_of(number_of, total, limit, lean, full):
    loads = [(1 << 20) // math.isqrt(rank ** lean) + 1 for rank in range(1, number_of + 1)]
    largest = limit if full else min(limit, max(-(-total // number_of), total * loads[0] // sum(loads)))
    least = 1 if total - largest >= number_of - 1 else 0
    counts, spare = [largest] + [least] * (number_of - 1), total - largest - least * (number_of - 1)
    while spare > 0:
        candidates = [i for i in range(1, number_of) if counts[i] < largest] or [i for i in range(1, number_of) if counts[i] < limit]
        pool, left = sum([loads[i] for i in candidates]), spare
        for i in candidates:
            extra = min(limit - counts[i], max(1, left * loads[i] // pool), spare)
            counts[i] = counts[i] + extra
            spare = spare - extra
    return np.array(counts)


def scatter_about(stream_key, dims, deviation, bound, shards=(), kind=jnp.bfloat16):
    gain = block_scale(stream_key, dims, shards, -0.22, 0.18) if shards else 1.0
    result = jax.random.normal(stream_key, dims, jnp.float32) * deviation * gain
    return jnp.minimum(jnp.maximum(result, -bound), bound).astype(kind)


def setup_inputs(seed: int = 0) -> dict:
    seeds = jax.random.split(jax.random.key(seed), 8)
    queries = draw_queries(jax.random.fold_in(seeds[7], 71), 0)
    ctx_keys = draw_ctx_keys(jax.random.fold_in(seeds[7], 71), 0)
    ctx_values = scatter_about(seeds[2], (CTX, KVH, D_HEAD), 1.0, 6.0, ((0, 32), (1, 4)))
    new_keys = draw_new_keys(jax.random.fold_in(seeds[7], 71), 0)
    new_values = scatter_about(seeds[4], (STRETCH, KVH, D_HEAD), 1.0, 6.0, ((0, 32), (1, 4)))
    picks_keys = jax.random.split(jax.random.fold_in(seeds[5], 1), KVH * NQB // QB_DEV)
    picks_turns = jax.random.permutation(jax.random.fold_in(seeds[5], 3), KVH * NQB // QB_DEV)
    picks = jax.vmap(lambda own, number: shared_out(jax.random.fold_in(seeds[5], 2), own, number, QB_DEV, NCTX, PICKS, CAP, 2))(picks_keys, picks_turns).reshape((KVH, NQB, PICKS))
    out_weight = scatter_about(seeds[6], (HQ * D_HEAD, DM), (HQ * D_HEAD) ** -0.5, 0.09375, ((0, 4),))
    return {"queries": queries, "ctx_keys": ctx_keys, "ctx_values": ctx_values, "new_keys": new_keys, "new_values": new_values, "picks": picks, "out_weight": out_weight}


NEGATIVE = -1.0e30


def attend(query_rows, key_rows, value_rows, allowed):
    score_scale = float(query_rows.shape[-1]) ** -0.5
    scores = jnp.dot(query_rows, key_rows.T, preferred_element_type=jnp.float32) * score_scale
    if allowed is not None:
        scores = jnp.where(allowed, scores, NEGATIVE)
    row_max = jnp.max(scores, axis=1, keepdims=True)
    exponent = jnp.exp(scores - row_max)
    if allowed is not None:
        exponent = jnp.where(allowed, exponent, 0.0)
    row_total = jnp.sum(exponent, axis=1)
    numerator = jnp.dot(exponent.astype(jnp.bfloat16), value_rows, preferred_element_type=jnp.float32)
    return numerator / row_total[:, None], row_max[:, 0] + jnp.log(row_total)


def reference(queries, ctx_keys, ctx_values, new_keys, new_values, picks, out_weight):
    group_size = HQ // KVH
    blocks = STRETCH // QB
    by_block = queries.reshape(blocks, QB, KVH, group_size, D_HEAD).transpose(2, 0, 1, 3, 4)
    by_block = by_block.reshape(KVH, blocks, QB * group_size, D_HEAD)
    keys_by_head = jnp.transpose(ctx_keys, (1, 0, 2))
    values_by_head = jnp.transpose(ctx_values, (1, 0, 2))

    def head_picks(operands):
        head_queries, head_keys, head_values, head_list = operands

        def block_picks(operand_pair):
            block_queries, block_list = operand_pair
            outputs = []
            lse_list = []
            for pick_index in range(PICKS):
                first_row = (block_list[pick_index] * KB).astype(jnp.int32)
                chosen_keys = lax.dynamic_slice_in_dim(head_keys, first_row, KB, 0)
                chosen_values = lax.dynamic_slice_in_dim(head_values, first_row, KB, 0)
                part_out, part_lse = attend(block_queries, chosen_keys, chosen_values, None)
                outputs.append(part_out)
                lse_list.append(part_lse)
            return jnp.stack(outputs), jnp.stack(lse_list)

        return lax.map(block_picks, (head_queries, head_list))

    pick_out, pick_lse = lax.map(head_picks, (by_block, keys_by_head, values_by_head, picks))
    pick_out = pick_out.reshape(KVH, blocks, PICKS, QB, group_size, D_HEAD).transpose(0, 1, 3, 4, 2, 5)
    pick_out = pick_out.reshape(KVH, STRETCH, group_size, PICKS, D_HEAD)
    pick_lse = pick_lse.reshape(KVH, blocks, PICKS, QB, group_size).transpose(0, 1, 3, 4, 2)
    pick_lse = pick_lse.reshape(KVH, STRETCH, group_size, PICKS)

    by_row = queries.reshape(STRETCH, KVH, group_size, D_HEAD).transpose(1, 0, 2, 3)
    new_keys_by_head = jnp.transpose(new_keys, (1, 0, 2))
    new_values_by_head = jnp.transpose(new_values, (1, 0, 2))
    step_rows = math.gcd(math.gcd(512, KB), STRETCH)
    window = min(KB, STRETCH)

    def head_own(operands):
        head_queries, head_keys, head_values = operands

        def row_block(block_index):
            first_row = block_index * step_rows
            window_start = (first_row // KB) * KB
            block_queries = lax.dynamic_slice_in_dim(head_queries, first_row, step_rows, 0)
            block_queries = block_queries.reshape(step_rows * group_size, D_HEAD)
            window_keys = lax.dynamic_slice_in_dim(head_keys, window_start, window, 0)
            window_values = lax.dynamic_slice_in_dim(head_values, window_start, window, 0)
            row_pos = first_row + jnp.arange(step_rows * group_size, dtype=jnp.int32) // group_size
            col_pos = window_start + jnp.arange(window, dtype=jnp.int32)
            allowed = col_pos[None, :] <= row_pos[:, None]
            return attend(block_queries, window_keys, window_values, allowed)

        return lax.map(row_block, jnp.arange(STRETCH // step_rows, dtype=jnp.int32))

    own_out, own_lse = lax.map(head_own, (by_row, new_keys_by_head, new_values_by_head))
    own_out = own_out.reshape(KVH, STRETCH, group_size, 1, D_HEAD)
    own_lse = own_lse.reshape(KVH, STRETCH, group_size, 1)

    all_out = jnp.concatenate([own_out, pick_out], axis=3)
    all_lse = jnp.concatenate([own_lse, pick_lse], axis=3)
    best = jnp.max(all_lse, axis=3, keepdims=True)
    shares = jnp.exp(all_lse - best)
    merged = jnp.sum(shares[..., None] * all_out, axis=3) / jnp.sum(shares, axis=3)[..., None]
    merged = merged.transpose(1, 0, 2, 3).reshape(STRETCH, HQ * D_HEAD).astype(jnp.bfloat16)
    return jnp.dot(merged, out_weight, preferred_element_type=jnp.float32).astype(jnp.bfloat16)
```

```python
import functools

import jax
import jax.numpy as jnp
from jax import lax
from jax.experimental import pallas as pl
from jax.experimental.pallas import tpu as pltpu
from jax.sharding import PartitionSpec as P

LOG2E = 1.4426950408889634
NT = (((1,), (1,)), ((), ()))
TN = (((0,), (0,)), ((), ()))
VM = pl.BlockSpec(memory_space=pltpu.VMEM)
SM = pl.BlockSpec(memory_space=pltpu.SMEM)
KB = 4096
BIG = 60 * 2**20
EXTRA = 16


def split_queries(rows):
    scale = LOG2E * float(rows.shape[-1]) ** -0.5
    scaled = rows.astype(jnp.float32) * scale
    high = scaled.astype(jnp.bfloat16)
    low = (scaled - high.astype(jnp.float32)).astype(jnp.bfloat16)
    return jnp.concatenate([high, low], axis=1)


def scores_of(keys, split):
    return lax.dot_general(
        jnp.concatenate([keys, keys], axis=1), split, NT, preferred_element_type=jnp.float32
    )


def attend_tile(rows, keys_at, values_t_at, chunks):
    split = split_queries(rows)
    top = total = acc = None
    now = scores_of(keys_at(0), split)
    for c in range(chunks):
        later = scores_of(keys_at(c + 1), split) if c + 1 < chunks else None
        best = jnp.max(now, axis=0, keepdims=True)
        best = best if top is None else jnp.maximum(top, best)
        e = jnp.exp2(now - best)
        part = jnp.sum(e, axis=0, keepdims=True)
        out = jnp.dot(values_t_at(c), e.astype(jnp.bfloat16), preferred_element_type=jnp.float32)
        if top is None:
            acc, total = out, part
        else:
            fade = jnp.exp2(top - best)
            acc, total = acc * fade + out, total * fade + part
        top, now = best, later
    return acc / total, top + jnp.log2(total)


def three_parts(row):
    high = row.astype(jnp.bfloat16).astype(jnp.float32)
    rest = row - high
    mid = rest.astype(jnp.bfloat16).astype(jnp.float32)
    fill = jnp.zeros((EXTRA - 3, row.shape[1]), jnp.float32)
    return jnp.concatenate([high, mid, rest - mid, fill], axis=0).astype(jnp.bfloat16)


def place_kernel(picks_ref, q_ref, out_ref, slot_ref, count_ref):
    heads, blocks, picked = picks_ref.shape
    item = q_ref.shape[1] // blocks
    owners = out_ref.shape[0]
    out_ref[...] = jnp.zeros_like(out_ref)

    def clear(i, _):
        for h in range(heads):
            count_ref[h, i] = 0
        return 0

    lax.fori_loop(0, owners, clear, 0)
    for h in range(heads):

        def one(q, _):
            rows = q_ref[h, pl.ds(pl.multiple_of(q * item, item), item), :]
            for p in range(picked):
                t = picks_ref[h, q, p]
                c = count_ref[h, t]
                count_ref[h, t] = c + 1
                slot_ref[h, q, p] = c
                out_ref[t, h, pl.ds(pl.multiple_of(c * item, item), item), :] = rows
            return 0

        lax.fori_loop(0, blocks, one, 0)


def place(picks, q):
    heads, rows, feature = q.shape
    return pl.pallas_call(
        place_kernel,
        out_shape=(
            jax.ShapeDtypeStruct((32, heads, 128, feature), jnp.bfloat16),
            jax.ShapeDtypeStruct(picks.shape, jnp.int32),
        ),
        in_specs=[SM, VM],
        out_specs=(VM, SM),
        scratch_shapes=[pltpu.SMEM((heads, 32), jnp.int32)],
        compiler_params=pltpu.CompilerParams(vmem_limit_bytes=BIG),
    )(picks, q)


def context_kernel(q_ref, k_ref, v_ref, out_ref):
    sources, heads, slot_rows, feature = q_ref.shape
    group, step = 4, 1024

    def tile(i, _):
        first = i * group
        for h in range(heads):
            rows = jnp.concatenate([q_ref[first + j, h] for j in range(group)], axis=0)
            out, lse = attend_tile(
                rows,
                lambda c: k_ref[h, c * step : (c + 1) * step, :],
                lambda c: v_ref[h, :, c * step : (c + 1) * step],
                KB // step,
            )
            out = out.T.astype(jnp.bfloat16)
            for j in range(group):
                cut = slice(j * slot_rows, (j + 1) * slot_rows)
                out_ref[first + j, h, 0:slot_rows, :] = out[cut, :]
                out_ref[first + j, h, slot_rows : slot_rows + EXTRA, :] = three_parts(lse[:, cut])
        return 0

    lax.fori_loop(0, sources // group, tile, 0)


def context(arrived, keys, values_t):
    sources, heads, slot_rows, feature = arrived.shape
    return pl.pallas_call(
        context_kernel,
        out_shape=jax.ShapeDtypeStruct((sources, heads, slot_rows + EXTRA, feature), jnp.bfloat16),
        in_specs=[VM, VM, VM],
        out_specs=VM,
        compiler_params=pltpu.CompilerParams(vmem_limit_bytes=BIG),
    )(arrived, keys, values_t)


def own_kernel(picks_ref, slot_ref, q_ref, kv_ref, ret_ref, out_ref, acc_ref, top_ref, sum_ref):
    heads, rows, feature = q_ref.shape
    blocks, picked = picks_ref.shape[1:]
    item = rows // blocks
    block_rows = out_ref.shape[0] // blocks
    group = item // block_rows
    span = kv_ref.shape[3]
    mine = lax.rem(lax.axis_index("seq"), kv_ref.shape[0])

    def absorb(j, masked):
        for h in range(heads):
            split = split_queries(q_ref[h])
            s = scores_of(kv_ref[j, 0, h], split)
            if masked:
                key_at = lax.broadcasted_iota(jnp.int32, s.shape, 0)
                col = lax.broadcasted_iota(jnp.int32, s.shape, 1)
                row_at = (col // item) * block_rows + lax.rem(col, block_rows)
                s = jnp.where(key_at <= row_at, s, -1e30)
            best = jnp.max(s, axis=0, keepdims=True)
            if not masked:
                best = jnp.maximum(top_ref[h, 0:1, :], best)
            e = jnp.exp2(s - best)
            part = jnp.sum(e, axis=0, keepdims=True)
            o = lax.dot_general(
                kv_ref[j, 1, h], e.astype(jnp.bfloat16), TN, preferred_element_type=jnp.float32
            )
            if masked:
                acc_ref[h] = o
                sum_ref[h, 0:1, :] = part
            else:
                fade = jnp.exp2(top_ref[h, 0:1, :] - best)
                acc_ref[h] = acc_ref[h] * fade + o
                sum_ref[h, 0:1, :] = sum_ref[h, 0:1, :] * fade + part
            top_ref[h, 0:1, :] = best

    absorb(mine, True)

    def step(j, _):
        absorb(j, False)
        return 0

    lax.fori_loop(0, mine, step, 0)
    for h in range(heads):
        total = sum_ref[h, 0:1, :]
        own = (acc_ref[h] / total).T
        lses = [top_ref[h, 0:1, :] + jnp.log2(total)]
        for p in range(picked):
            pieces = []
            for q in range(blocks):
                t, c = picks_ref[h, q, p], slot_ref[h, q, p]
                lse = jnp.sum(
                    ret_ref[t, h, 2 * item : 2 * item + EXTRA, :].astype(jnp.float32),
                    axis=0,
                    keepdims=True,
                )
                pieces.append(jnp.where(c == 0, lse[:, 0:item], lse[:, item : 2 * item]))
            lses.append(jnp.concatenate(pieces, axis=1))
        best = functools.reduce(jnp.maximum, lses)
        shares = [jnp.exp2(x - best) for x in lses]
        whole = functools.reduce(jnp.add, shares)
        shares = [x / whole for x in shares]
        fill = [jnp.zeros_like(best)] * (8 - len(shares))
        columns = jnp.concatenate(shares + fill, axis=0).T
        for q in range(blocks):
            cut = slice(q * item, (q + 1) * item)
            mix = own[cut, :] * columns[cut, 0:1]
            for p in range(picked):
                t, c = picks_ref[h, q, p], slot_ref[h, q, p]
                got = ret_ref[t, h, pl.ds(pl.multiple_of(c * item, item), item), :]
                mix = mix + got.astype(jnp.float32) * columns[cut, p + 1 : p + 2]
            mix = mix.astype(jnp.bfloat16)
            for g in range(group):
                at = (h * group + g) * feature
                out_ref[q * block_rows : (q + 1) * block_rows, at : at + feature] = mix[
                    g * block_rows : (g + 1) * block_rows, :
                ]


def own_and_merge(picks, slots, q, kv, ret):
    heads, rows, feature = q.shape
    return pl.pallas_call(
        own_kernel,
        out_shape=jax.ShapeDtypeStruct((256, 8 * feature), jnp.bfloat16),
        in_specs=[SM, SM, VM, VM, VM],
        out_specs=VM,
        scratch_shapes=[
            pltpu.VMEM((heads, feature, rows), jnp.float32),
            pltpu.VMEM((heads, 8, rows), jnp.float32),
            pltpu.VMEM((heads, 8, rows), jnp.float32),
        ],
        compiler_params=pltpu.CompilerParams(vmem_limit_bytes=BIG),
    )(picks, slots, q, kv, ret)


def on_device(queries, ctx_keys, ctx_values, new_keys, new_values, picks, out_weight):
    q = queries.reshape(16, 16, 2, 4, 128).transpose(2, 0, 3, 1, 4).reshape(2, 1024, 128)
    outgoing, slots = place(picks, q)
    arrived = lax.all_to_all(outgoing, "seq", split_axis=0, concat_axis=0, tiled=True)
    keys = ctx_keys.transpose(1, 0, 2)
    values_t = ctx_values.transpose(1, 2, 0)
    kv = jnp.stack([new_keys.transpose(1, 0, 2), new_values.transpose(1, 0, 2)])
    groups = [list(range(16)), list(range(16, 32))]
    kv = lax.all_gather(kv, "seq", axis=0, axis_index_groups=groups)
    done = context(arrived, keys, values_t)
    ret = lax.all_to_all(done, "seq", split_axis=0, concat_axis=0, tiled=True)
    merged = own_and_merge(picks, slots, q, kv, ret)
    return lax.psum_scatter(
        jnp.dot(merged, out_weight, preferred_element_type=jnp.float32).astype(jnp.bfloat16),
        "kvh",
        scatter_dimension=0,
        tiled=True,
    )


def solution(mesh):
    placed = (
        P("seq", "kvh", None),
        P("seq", "kvh", None),
        P("seq", "kvh", None),
        P("seq", "kvh", None),
        P("seq", "kvh", None),
        P("kvh", "seq", None),
        P("kvh", None),
    )
    return jax.shard_map(
        on_device, mesh=mesh, in_specs=placed, out_specs=P(("seq", "kvh"), None), check_vma=False
    )
```

```python
import functools

import jax
import jax.numpy as jnp
from jax import lax
from jax.experimental import pallas as pl
from jax.experimental.pallas import tpu as pltpu
from jax.sharding import PartitionSpec as P

LOG2E = 1.4426950408889634
NT = (((1,), (1,)), ((), ()))
VM = pl.BlockSpec(memory_space=pltpu.VMEM)
SM = pl.BlockSpec(memory_space=pltpu.SMEM)
KB = 4096
BIG = 60 * 2**20
EXTRA = 16
LAG = 2
MESH = pl.DeviceIdType.MESH
ANY = pl.BlockSpec(memory_space=pl.ANY)


def split_queries(rows):
    scale = LOG2E * float(rows.shape[-1]) ** -0.5
    scaled = rows.astype(jnp.float32) * scale
    high = scaled.astype(jnp.bfloat16)
    low = (scaled - high.astype(jnp.float32)).astype(jnp.bfloat16)
    return jnp.concatenate([high, low], axis=1)


def scores_of(keys, split):
    return lax.dot_general(
        jnp.concatenate([keys, keys], axis=1), split, NT, preferred_element_type=jnp.float32
    )


def attend_tile(rows, keys_at, values_t_at, chunks):
    split = split_queries(rows)
    top = total = acc = None
    now = scores_of(keys_at(0), split)
    for c in range(chunks):
        later = scores_of(keys_at(c + 1), split) if c + 1 < chunks else None
        best = jnp.max(now, axis=0, keepdims=True)
        best = best if top is None else jnp.maximum(top, best)
        e = jnp.exp2(now - best)
        part = jnp.sum(e, axis=0, keepdims=True)
        out = jnp.dot(values_t_at(c), e.astype(jnp.bfloat16), preferred_element_type=jnp.float32)
        if top is None:
            acc, total = out, part
        else:
            fade = jnp.exp2(top - best)
            acc, total = acc * fade + out, total * fade + part
        top, now = best, later
    return acc / total, top + jnp.log2(total)


def three_parts(row):
    high = row.astype(jnp.bfloat16).astype(jnp.float32)
    rest = row - high
    mid = rest.astype(jnp.bfloat16).astype(jnp.float32)
    fill = jnp.zeros((EXTRA - 3, row.shape[1]), jnp.float32)
    return jnp.concatenate([high, mid, rest - mid, fill], axis=0).astype(jnp.bfloat16)


def place_kernel(picks_ref, q_ref, out_ref, slot_ref, count_ref):
    heads, blocks, picked = picks_ref.shape
    item = q_ref.shape[1] // blocks
    owners = out_ref.shape[0]
    out_ref[...] = jnp.zeros_like(out_ref)

    def clear(i, _):
        for h in range(heads):
            count_ref[h, i] = 0
        return 0

    lax.fori_loop(0, owners, clear, 0)
    for h in range(heads):

        def one(q, _):
            rows = q_ref[h, pl.ds(pl.multiple_of(q * item, item), item), :]
            for p in range(picked):
                t = picks_ref[h, q, p]
                c = count_ref[h, t]
                count_ref[h, t] = c + 1
                slot_ref[h, q, p] = c
                out_ref[t, h, pl.ds(pl.multiple_of(c * item, item), item), :] = rows
            return 0

        lax.fori_loop(0, blocks, one, 0)


def place(picks, q):
    heads, rows, feature = q.shape
    return pl.pallas_call(
        place_kernel,
        out_shape=(
            jax.ShapeDtypeStruct((32, heads, 128, feature), jnp.bfloat16),
            jax.ShapeDtypeStruct(picks.shape, jnp.int32),
        ),
        in_specs=[SM, VM],
        out_specs=(VM, SM),
        scratch_shapes=[pltpu.SMEM((heads, 32), jnp.int32)],
        compiler_params=pltpu.CompilerParams(vmem_limit_bytes=BIG),
    )(picks, q)


def exchange_kernel(
    out_ref, key_ref, value_ref, q_ref, kv_ref, ret, own_ref, lse_ref,
    keys, values, arrived, done, kvs, acc_ref, top_ref, sum_ref,
    load_sem, send_sem, recv_sem, back_sem, home_sem, kv_send, kv_recv,
):
    owners, heads, slot_rows, feature = out_ref.shape
    spans = kvs.shape[0]
    me = lax.axis_index("seq")
    mine = lax.rem(me, spans)
    group, step = 4, 1024

    loads = [
        pltpu.make_async_copy(key_ref, keys, load_sem.at[0]),
        pltpu.make_async_copy(value_ref, values, load_sem.at[1]),
    ]
    for load in loads:
        load.start()
    barrier = pltpu.get_barrier_semaphore()

    def greet(d, _):
        pl.semaphore_signal(
            barrier, inc=1, device_id={"seq": lax.rem(me + d, owners)}, device_id_type=MESH
        )
        return 0

    lax.fori_loop(1, owners, greet, 0)
    pl.semaphore_wait(barrier, owners - 1)

    def outward(d):
        to = lax.rem(me + d, owners)
        return pltpu.make_async_remote_copy(
            src_ref=out_ref.at[to],
            dst_ref=arrived.at[d],
            send_sem=send_sem.at[d],
            recv_sem=recv_sem.at[d],
            device_id={"seq": to},
            device_id_type=MESH,
        )

    def homeward(d):
        return pltpu.make_async_remote_copy(
            src_ref=done.at[d],
            dst_ref=ret.at[d],
            send_sem=back_sem.at[d],
            recv_sem=home_sem.at[d],
            device_id={"seq": lax.rem(me - d + owners, owners)},
            device_id_type=MESH,
        )

    def kv_copy(d):
        return pltpu.make_async_remote_copy(
            src_ref=kv_ref,
            dst_ref=kvs.at[d],
            send_sem=kv_send.at[d],
            recv_sem=kv_recv.at[d],
            device_id={"seq": lax.rem(me + d, owners)},
            device_id_type=MESH,
        )

    def start_out(d, _):
        outward(d).start()
        return 0

    lax.fori_loop(1, owners, start_out, 0)

    def start_kv(d, _):
        kv_copy(d).start()
        return 0

    lax.fori_loop(1, spans - mine, start_kv, 0)
    arrived[0] = out_ref[me]
    for load in loads:
        load.wait()

    def tile(i, _):
        first = i * group
        for j in range(group):
            if j == 0:

                @pl.when(i > 0)
                def _():
                    outward(first).wait_recv()

            else:
                outward(first + j).wait_recv()
        for h in range(heads):
            rows = jnp.concatenate([arrived[first + j, h] for j in range(group)], axis=0)
            out, lse = attend_tile(
                rows,
                lambda c: keys[h, c * step : (c + 1) * step, :],
                lambda c: values[h, :, c * step : (c + 1) * step],
                KB // step,
            )
            out = out.T.astype(jnp.bfloat16)
            for j in range(group):
                cut = slice(j * slot_rows, (j + 1) * slot_rows)
                done[first + j, h, 0:slot_rows, :] = out[cut, :]
                done[first + j, h, slot_rows : slot_rows + EXTRA, :] = three_parts(lse[:, cut])
        for j in range(group):
            if j == 0:

                @pl.when(i > 0)
                def _():
                    homeward(first).start()

            else:
                homeward(first + j).start()
        return 0

    lax.fori_loop(0, owners // group, tile, 0)
    ret[0] = done[0]

    item = slot_rows // 2
    block_rows = item // 4
    half = kv_ref.shape[2] // 2

    def absorb(pairs, first):
        for h in range(heads):
            split = split_queries(q_ref[h])
            key_rows = [ref[0, h] for ref in pairs]
            key_rows = key_rows[0] if len(pairs) == 1 else jnp.concatenate(key_rows, axis=0)
            value_t = jnp.concatenate(
                [ref[1, h, x : x + half, :] for ref in pairs for x in (0, half)], axis=1
            )
            s = scores_of(key_rows, split)
            if first:
                key_at = lax.broadcasted_iota(jnp.int32, s.shape, 0)
                col = lax.broadcasted_iota(jnp.int32, s.shape, 1)
                row_at = (col // item) * block_rows + lax.rem(col, block_rows)
                s = jnp.where(key_at <= row_at, s, -1e30)
            best = jnp.max(s, axis=0, keepdims=True)
            if not first:
                best = jnp.maximum(top_ref[h, 0:1, :], best)
            e = jnp.exp2(s - best)
            part = jnp.sum(e, axis=0, keepdims=True)
            o = jnp.dot(value_t, e.astype(jnp.bfloat16), preferred_element_type=jnp.float32)
            if first:
                acc_ref[h] = o
                sum_ref[h, 0:1, :] = part
            else:
                fade = jnp.exp2(top_ref[h, 0:1, :] - best)
                acc_ref[h] = acc_ref[h] * fade + o
                sum_ref[h, 0:1, :] = sum_ref[h, 0:1, :] * fade + part
            top_ref[h, 0:1, :] = best

    absorb([kv_ref], True)

    def two(j, _):
        d = 2 * j + 1
        kv_copy(d).wait_recv()
        kv_copy(d + 1).wait_recv()
        absorb([kvs.at[d], kvs.at[d + 1]], False)
        return 0

    lax.fori_loop(0, mine // 2, two, 0)

    @pl.when(lax.rem(mine, 2) == 1)
    def _():
        kv_copy(mine).wait_recv()
        absorb([kvs.at[mine]], False)

    def finish(d, _):
        homeward(d).wait_recv()
        outward(d).wait_send()
        homeward(d).wait_send()
        return 0

    lax.fori_loop(1, owners, finish, 0)

    def finish_kv(d, _):
        kv_copy(d).wait_send()
        return 0

    lax.fori_loop(1, spans - mine, finish_kv, 0)

    for h in range(heads):
        total = sum_ref[h, 0:1, :]
        own_ref[h] = (acc_ref[h] / total).T
        lse_ref[h] = jnp.broadcast_to(top_ref[h, 0:1, :] + jnp.log2(total), lse_ref.shape[1:])


def merge_kernel(picks_ref, slot_ref, own_ref, own_lse_ref, ret, merged_ref):
    owners, heads = ret.shape[:2]
    feature = own_ref.shape[2]
    blocks, picked = picks_ref.shape[1:]
    item = own_ref.shape[1] // blocks
    block_rows = merged_ref.shape[0] // blocks
    fold = item // block_rows
    me = lax.axis_index("seq")
    for h in range(heads):
        own = own_ref[h]
        lses = [own_lse_ref[h, 0:1, :]]
        for p in range(picked):
            pieces = []
            for b in range(blocks):
                at, c = lax.rem(picks_ref[h, b, p] - me + owners, owners), slot_ref[h, b, p]
                lse = jnp.sum(
                    ret[at, h, 2 * item : 2 * item + EXTRA, :].astype(jnp.float32),
                    axis=0,
                    keepdims=True,
                )
                pieces.append(jnp.where(c == 0, lse[:, 0:item], lse[:, item : 2 * item]))
            lses.append(jnp.concatenate(pieces, axis=1))
        best = functools.reduce(jnp.maximum, lses)
        shares = [jnp.exp2(x - best) for x in lses]
        whole = functools.reduce(jnp.add, shares)
        shares = [x / whole for x in shares]
        fill = [jnp.zeros_like(best)] * (8 - len(shares))
        columns = jnp.concatenate(shares + fill, axis=0).T
        for b in range(blocks):
            cut = slice(b * item, (b + 1) * item)
            mix = own[cut, :] * columns[cut, 0:1]
            for p in range(picked):
                at, c = lax.rem(picks_ref[h, b, p] - me + owners, owners), slot_ref[h, b, p]
                got = ret[at, h, pl.ds(pl.multiple_of(c * item, item), item), :]
                mix = mix + got.astype(jnp.float32) * columns[cut, p + 1 : p + 2]
            mix = mix.astype(jnp.bfloat16)
            for g in range(fold):
                lane = (h * fold + g) * feature
                merged_ref[b * block_rows : (b + 1) * block_rows, lane : lane + feature] = mix[
                    g * block_rows : (g + 1) * block_rows, :
                ]


def merge(picks, slots, own, lse, ret):
    return pl.pallas_call(
        merge_kernel,
        out_shape=jax.ShapeDtypeStruct((256, 8 * own.shape[2]), jnp.bfloat16),
        in_specs=[SM, SM, VM, VM, VM],
        out_specs=VM,
        compiler_params=pltpu.CompilerParams(vmem_limit_bytes=BIG),
    )(picks, slots, own, lse, ret)


def exchange(outgoing, keys, values_t, q, kv):
    owners, heads, slot_rows, feature = outgoing.shape
    rows = q.shape[1]
    back = (owners, heads, slot_rows + EXTRA, feature)
    dma = pltpu.SemaphoreType.DMA
    return pl.pallas_call(
        exchange_kernel,
        out_shape=(
            jax.ShapeDtypeStruct(back, jnp.bfloat16),
            jax.ShapeDtypeStruct((heads, rows, feature), jnp.float32),
            jax.ShapeDtypeStruct((heads, 8, rows), jnp.float32),
        ),
        in_specs=[VM, ANY, ANY, VM, VM],
        out_specs=(VM, VM, VM),
        scratch_shapes=[
            pltpu.VMEM(keys.shape, jnp.bfloat16),
            pltpu.VMEM(values_t.shape, jnp.bfloat16),
            pltpu.VMEM(outgoing.shape, jnp.bfloat16),
            pltpu.VMEM(back, jnp.bfloat16),
            pltpu.VMEM((16,) + kv.shape, jnp.bfloat16),
            pltpu.VMEM((heads, feature, rows), jnp.float32),
            pltpu.VMEM((heads, 8, rows), jnp.float32),
            pltpu.VMEM((heads, 8, rows), jnp.float32),
            dma((2,)),
            dma((owners,)),
            dma((owners,)),
            dma((owners,)),
            dma((owners,)),
            dma((16,)),
            dma((16,)),
        ],
        compiler_params=pltpu.CompilerParams(
            collective_id=0, has_side_effects=True, vmem_limit_bytes=BIG
        ),
    )(outgoing, keys, values_t, q, kv)


def project_kernel(
    m_ref, w_ref, out_ref, w_buf, order, sent1, keep, got1, sent2, mine2, got2,
    load_sem, send1, recv1, send2, recv2,
):
    parts, depth, wide = w_buf.shape
    y = lax.axis_index("kvh")
    beside = y + 1 - 2 * lax.rem(y, 2)
    across = 3 - y
    far = 3 - beside
    rows = m_ref.shape[0] // 4

    loads = [
        pltpu.make_async_copy(w_ref.at[:, n * wide : (n + 1) * wide], w_buf.at[n], load_sem.at[n])
        for n in range(parts)
    ]
    for load in loads:
        load.start()
    barrier = pltpu.get_barrier_semaphore()
    for other in (beside, across):
        pl.semaphore_signal(barrier, inc=1, device_id={"kvh": other}, device_id_type=MESH)
    for kind, blocks in enumerate(((beside, far, across, y), (across, far, beside, y))):
        for i, b in enumerate(blocks):
            order[kind, i * rows : (i + 1) * rows, :] = m_ref[
                pl.ds(pl.multiple_of(b * rows, rows), rows), :
            ]
    pl.semaphore_wait(barrier, 2)

    def first_copy(n):
        return pltpu.make_async_remote_copy(
            src_ref=sent1.at[n],
            dst_ref=got1.at[n],
            send_sem=send1.at[n],
            recv_sem=recv1.at[n],
            device_id={"kvh": beside if n % 2 == 0 else across},
            device_id_type=MESH,
        )

    def second_copy(n):
        return pltpu.make_async_remote_copy(
            src_ref=sent2.at[n],
            dst_ref=got2.at[n],
            send_sem=send2.at[n],
            recv_sem=recv2.at[n],
            device_id={"kvh": across if n % 2 == 0 else beside},
            device_id_type=MESH,
        )

    def forward(n):
        first_copy(n).wait_recv()
        both = got1[n].astype(jnp.float32)
        sent2[n] = (keep[n, 0:rows, :] + both[rows:, :]).astype(jnp.bfloat16)
        mine2[n] = keep[n, rows:, :] + both[0:rows, :]
        second_copy(n).start()

    for n in range(parts):
        loads[n].wait()
        product = jnp.dot(order[n % 2], w_buf[n], preferred_element_type=jnp.float32)
        sent1[n] = product[0 : 2 * rows, :].astype(jnp.bfloat16)
        keep[n] = product[2 * rows :, :]
        first_copy(n).start()
        if n >= LAG:
            forward(n - LAG)
    for n in range(parts - LAG, parts):
        forward(n)
    for n in range(parts):
        second_copy(n).wait_recv()
        out_ref[:, n * wide : (n + 1) * wide] = (
            mine2[n] + got2[n].astype(jnp.float32)
        ).astype(jnp.bfloat16)
    for n in range(parts):
        first_copy(n).wait_send()
        second_copy(n).wait_send()


def project(merged, weight):
    rows, depth = merged.shape
    width = weight.shape[1]
    parts = 8
    wide = width // parts
    quarter = rows // 4
    dma = pltpu.SemaphoreType.DMA
    return pl.pallas_call(
        project_kernel,
        out_shape=jax.ShapeDtypeStruct((quarter, width), jnp.bfloat16),
        in_specs=[VM, ANY],
        out_specs=VM,
        scratch_shapes=[
            pltpu.VMEM((parts, depth, wide), jnp.bfloat16),
            pltpu.VMEM((2, rows, depth), jnp.bfloat16),
            pltpu.VMEM((parts, 2 * quarter, wide), jnp.bfloat16),
            pltpu.VMEM((parts, 2 * quarter, wide), jnp.float32),
            pltpu.VMEM((parts, 2 * quarter, wide), jnp.bfloat16),
            pltpu.VMEM((parts, quarter, wide), jnp.bfloat16),
            pltpu.VMEM((parts, quarter, wide), jnp.float32),
            pltpu.VMEM((parts, quarter, wide), jnp.bfloat16),
            dma((parts,)),
            dma((parts,)),
            dma((parts,)),
            dma((parts,)),
            dma((parts,)),
        ],
        compiler_params=pltpu.CompilerParams(
            collective_id=1, has_side_effects=True, vmem_limit_bytes=BIG
        ),
    )(merged, weight)


def on_device(queries, ctx_keys, ctx_values, new_keys, new_values, picks, out_weight):
    q = queries.reshape(16, 16, 2, 4, 128).transpose(2, 0, 3, 1, 4).reshape(2, 1024, 128)
    outgoing, slots = place(picks, q)
    keys = ctx_keys.transpose(1, 0, 2)
    values_t = ctx_values.transpose(1, 2, 0)
    new_t = new_values.reshape(2, 128, 2, 128).transpose(2, 0, 3, 1).reshape(2, 256, 128)
    kv = jnp.stack([new_keys.transpose(1, 0, 2), new_t])
    ret, own, lse = exchange(outgoing, keys, values_t, q, kv)
    merged = merge(picks, slots, own, lse, ret)
    return project(merged, out_weight)


def solution(mesh):
    placed = (
        P("seq", "kvh", None),
        P("seq", "kvh", None),
        P("seq", "kvh", None),
        P("seq", "kvh", None),
        P("seq", "kvh", None),
        P("kvh", "seq", None),
        P("kvh", None),
    )
    return jax.shard_map(
        on_device, mesh=mesh, in_specs=placed, out_specs=P(("seq", "kvh"), None), check_vma=False
    )
```

```python
import functools

import jax
import jax.numpy as jnp
from jax import lax
from jax.experimental import pallas as pl
from jax.experimental.pallas import tpu as pltpu
from jax.sharding import PartitionSpec as P

LOG2E = 1.4426950408889634
NT = (((1,), (1,)), ((), ()))
TN = (((0,), (0,)), ((), ()))
VM = pl.BlockSpec(memory_space=pltpu.VMEM)
SM = pl.BlockSpec(memory_space=pltpu.SMEM)
KB = 4096
BIG = 60 * 2**20
EXTRA = 16
LAG = 2
MESH = pl.DeviceIdType.MESH
ANY = pl.BlockSpec(memory_space=pl.ANY)


def split_queries(rows):
    scale = LOG2E * float(rows.shape[-1]) ** -0.5
    scaled = rows.astype(jnp.float32) * scale
    high = scaled.astype(jnp.bfloat16)
    low = (scaled - high.astype(jnp.float32)).astype(jnp.bfloat16)
    return jnp.concatenate([high, low], axis=1)


def scores_of(keys, split):
    return lax.dot_general(
        jnp.concatenate([keys, keys], axis=1), split, NT, preferred_element_type=jnp.float32
    )


def attend_tile(rows, keys_at, values_t_at, chunks):
    split = split_queries(rows)
    top = total = acc = None
    now = scores_of(keys_at(0), split)
    for c in range(chunks):
        later = scores_of(keys_at(c + 1), split) if c + 1 < chunks else None
        best = jnp.max(now, axis=0, keepdims=True)
        best = best if top is None else jnp.maximum(top, best)
        e = jnp.exp2(now - best)
        part = jnp.sum(e, axis=0, keepdims=True)
        out = jnp.dot(values_t_at(c), e.astype(jnp.bfloat16), preferred_element_type=jnp.float32)
        if top is None:
            acc, total = out, part
        else:
            fade = jnp.exp2(top - best)
            acc, total = acc * fade + out, total * fade + part
        top, now = best, later
    return acc / total, top + jnp.log2(total)


def three_parts(rows):
    parts = []
    for row in rows:
        high = row.astype(jnp.bfloat16).astype(jnp.float32)
        rest = row - high
        mid = rest.astype(jnp.bfloat16).astype(jnp.float32)
        parts += [high, mid, rest - mid]
    fill = jnp.zeros((EXTRA - len(parts), rows[0].shape[1]), jnp.float32)
    return jnp.concatenate(parts + [fill], axis=0).astype(jnp.bfloat16)


CHIPS = (
    ((0, 0), (0, 1)), ((1, 0), (0, 3)), ((3, 0), (1, 1)), ((3, 3), (1, 3)),
    ((3, 1), (0, 2)), ((2, 0), (1, 2)), ((2, 1), (3, 2)), ((2, 3), (2, 2)),
)
DIGITS = tuple(
    sum(pair[a][b] * 4**i for i, pair in enumerate(CHIPS)) for a in range(2) for b in range(2)
)


def offsets_of(digits):
    za, xa, zb, xb = [lax.rem(x, 4) for x in digits]
    return ((za, xa, 0), (za, xa, 1), (zb, xb, 0), (zb, xb, 1))


def next_digits(digits):
    return tuple(lax.div(x, 4) for x in digits)


def first_digits():
    return tuple(jnp.int32(x) for x in DIGITS)


def place_kernel(picks_ref, q_ref, out_ref, slot_ref, count_ref):
    heads, blocks, picked = picks_ref.shape
    item = q_ref.shape[1] // blocks
    owners = out_ref.shape[0]
    out_ref[...] = jnp.zeros_like(out_ref)

    def clear(i, _):
        for h in range(heads):
            count_ref[h, i] = 0
        return 0

    lax.fori_loop(0, owners, clear, 0)
    for h in range(heads):

        def one(q, _):
            rows = q_ref[h, pl.ds(pl.multiple_of(q * item, item), item), :]
            for p in range(picked):
                t = picks_ref[h, q, p]
                c = count_ref[h, t]
                count_ref[h, t] = c + 1
                slot_ref[h, q, p] = c
                out_ref[t, h, pl.ds(pl.multiple_of(c * item, item), item), :] = rows
            return 0

        lax.fori_loop(0, blocks, one, 0)


def place(picks, q):
    heads, rows, feature = q.shape
    return pl.pallas_call(
        place_kernel,
        out_shape=(
            jax.ShapeDtypeStruct((32, heads, 128, feature), jnp.bfloat16),
            jax.ShapeDtypeStruct(picks.shape, jnp.int32),
        ),
        in_specs=[SM, VM],
        out_specs=(VM, SM),
        scratch_shapes=[pltpu.SMEM((heads, 32), jnp.int32)],
        compiler_params=pltpu.CompilerParams(vmem_limit_bytes=BIG),
    )(picks, q)


def exchange_kernel(
    out_ref, key_ref, value_ref, q_ref, kv_ref, ret, own_ref, lse_ref,
    raw, keys, values, arrived, done, kvs, acc_ref, top_ref, sum_ref,
    load_sem, send_sem, recv_sem, back_sem, home_sem, kv_send, kv_recv, fwd_send, fwd_recv,
):
    owners, heads, slot_rows, feature = out_ref.shape
    me = lax.axis_index("seq")
    z, x, core = lax.div(me, 8), lax.rem(lax.div(me, 2), 4), lax.rem(me, 2)
    sibling = me + 1 - 2 * core
    place = lax.rem(z, 2) * 4 + x
    group, step = 4, 1024

    loads = [
        pltpu.make_async_copy(key_ref, raw.at[0], load_sem.at[0]),
        pltpu.make_async_copy(value_ref, raw.at[1], load_sem.at[1]),
    ]
    for load in loads:
        load.start()
    barrier = pltpu.get_barrier_semaphore()

    def greet(d, _):
        pl.semaphore_signal(
            barrier, inc=1, device_id={"seq": lax.rem(me + d, owners)}, device_id_type=MESH
        )
        return 0

    lax.fori_loop(1, owners, greet, 0)

    def ahead(offset):
        dz, dx, dc = offset
        return lax.rem(z + dz, 4) * 8 + lax.rem(x + dx, 4) * 2 + lax.rem(core + dc, 2)

    def behind(offset):
        dz, dx, dc = offset
        return lax.rem(z + 4 - dz, 4) * 8 + lax.rem(x + 4 - dx, 4) * 2 + lax.rem(core + dc, 2)

    def outward(k, to):
        return pltpu.make_async_remote_copy(
            src_ref=out_ref.at[to],
            dst_ref=arrived.at[k],
            send_sem=send_sem.at[k],
            recv_sem=recv_sem.at[k],
            device_id={"seq": to},
            device_id_type=MESH,
        )

    def homeward(k, to):
        return pltpu.make_async_remote_copy(
            src_ref=done.at[k],
            dst_ref=ret.at[k],
            send_sem=back_sem.at[k],
            recv_sem=home_sem.at[k],
            device_id={"seq": to},
            device_id_type=MESH,
        )

    def kv_copy(d):
        return pltpu.make_async_remote_copy(
            src_ref=kv_ref,
            dst_ref=kvs.at[2 * d + core],
            send_sem=kv_send.at[d],
            recv_sem=kv_recv.at[d],
            device_id={"seq": lax.rem(me + 2 * d, owners)},
            device_id_type=MESH,
        )

    def kv_beside():
        return pltpu.make_async_remote_copy(
            src_ref=kv_ref,
            dst_ref=kvs.at[0],
            send_sem=kv_send.at[0],
            recv_sem=kv_recv.at[0],
            device_id={"seq": sibling},
            device_id_type=MESH,
        )

    def kv_forward(d, from_core):
        return pltpu.make_async_remote_copy(
            src_ref=kvs.at[2 * d + from_core],
            dst_ref=kvs.at[2 * d + from_core],
            send_sem=fwd_send.at[d],
            recv_sem=fwd_recv.at[d],
            device_id={"seq": sibling},
            device_id_type=MESH,
        )

    span = 2 * feature
    row = lax.broadcasted_iota(jnp.int32, (span, span), 0)
    col = lax.broadcasted_iota(jnp.int32, (span, span), 1)
    picking = (col == 2 * lax.rem(row, feature) + lax.div(row, feature)).astype(jnp.bfloat16)
    placing = (row == 2 * lax.rem(col, feature) + lax.div(col, feature)).astype(jnp.bfloat16)

    pl.semaphore_wait(barrier, owners - 1)

    def start_out(i, digits):
        for j, offset in enumerate(offsets_of(digits)):
            k = i * group + j
            if j == 0:

                @pl.when(i > 0)
                def _():
                    outward(k, ahead(offset)).start()

            else:
                outward(k, ahead(offset)).start()
        return next_digits(digits)

    lax.fori_loop(0, owners // group, start_out, first_digits())

    def start_kv(d, _):
        kv_copy(d).start()
        return 0

    lax.fori_loop(1, 8 - place, start_kv, 0)

    @pl.when(core == 0)
    def _():
        kv_beside().start()

    arrived[0] = out_ref[me]
    loads[0].wait()

    def sort_keys(j, _):
        block = raw[0, pl.ds(pl.multiple_of(j * span, span), span), :]
        both = jnp.dot(picking, block, preferred_element_type=jnp.float32).astype(jnp.bfloat16)
        for h in range(heads):
            keys[h, pl.ds(pl.multiple_of(j * feature, feature), feature), :] = both[
                h * feature : (h + 1) * feature, :
            ]
        return 0

    lax.fori_loop(0, KB // feature, sort_keys, 0, unroll=4)
    loads[1].wait()

    def sort_values(j, _):
        block = raw[1, pl.ds(pl.multiple_of(j * span, span), span), :]
        both = lax.dot_general(block, placing, TN, preferred_element_type=jnp.float32)
        both = both.astype(jnp.bfloat16)
        for h in range(heads):
            values[h, :, pl.ds(pl.multiple_of(j * feature, feature), feature)] = both[
                :, h * feature : (h + 1) * feature
            ]
        return 0

    lax.fori_loop(0, KB // feature, sort_values, 0, unroll=4)

    def tile(i, digits):
        first = i * group
        offsets = offsets_of(digits)
        for j, offset in enumerate(offsets):
            if j == 0:

                @pl.when(i > 0)
                def _():
                    outward(first, sibling).wait_recv()

            else:
                outward(first + j, sibling).wait_recv()
        lses = []
        for h in range(heads):
            rows = jnp.concatenate([arrived[first + j, h] for j in range(group)], axis=0)
            out, lse = attend_tile(
                rows,
                lambda c: keys[h, c * step : (c + 1) * step, :],
                lambda c: values[h, :, c * step : (c + 1) * step],
                KB // step,
            )
            out = out.T.astype(jnp.bfloat16)
            lses.append(lse)
            for j in range(group):
                cut = slice(j * slot_rows, (j + 1) * slot_rows)
                done[first + j, h * slot_rows : (h + 1) * slot_rows, :] = out[cut, :]
        for j, offset in enumerate(offsets):
            cut = slice(j * slot_rows, (j + 1) * slot_rows)
            done[first + j, heads * slot_rows : heads * slot_rows + EXTRA, :] = three_parts(
                [lse[:, cut] for lse in lses]
            )
            if j == 0:

                @pl.when(i > 0)
                def _():
                    homeward(first, behind(offset)).start()

            else:
                homeward(first + j, behind(offset)).start()
        return next_digits(digits)

    lax.fori_loop(0, owners // group, tile, first_digits())
    ret[0] = done[0]

    item = slot_rows // 2
    block_rows = item // 4
    half = kv_ref.shape[2] // 2

    def pass_on(d, _):
        kv_copy(d).wait_recv()
        kv_forward(d, core).start()
        return 0

    lax.fori_loop(1, place + 1, pass_on, 0)

    def absorb(pairs, first):
        for h in range(heads):
            split = split_queries(q_ref[h])
            key_rows = [ref[0, h] for ref in pairs]
            key_rows = key_rows[0] if len(pairs) == 1 else jnp.concatenate(key_rows, axis=0)
            value_t = jnp.concatenate(
                [ref[1, h, at : at + half, :] for ref in pairs for at in (0, half)], axis=1
            )
            s = scores_of(key_rows, split)
            if first:
                key_at = lax.broadcasted_iota(jnp.int32, s.shape, 0)
                lane = lax.broadcasted_iota(jnp.int32, s.shape, 1)
                row_at = (lane // item) * block_rows + lax.rem(lane, block_rows)
                s = jnp.where(key_at <= row_at, s, -1e30)
            best = jnp.max(s, axis=0, keepdims=True)
            if not first:
                best = jnp.maximum(top_ref[h, 0:1, :], best)
            e = jnp.exp2(s - best)
            part = jnp.sum(e, axis=0, keepdims=True)
            o = jnp.dot(value_t, e.astype(jnp.bfloat16), preferred_element_type=jnp.float32)
            if first:
                acc_ref[h] = o
                sum_ref[h, 0:1, :] = part
            else:
                fade = jnp.exp2(top_ref[h, 0:1, :] - best)
                acc_ref[h] = acc_ref[h] * fade + o
                sum_ref[h, 0:1, :] = sum_ref[h, 0:1, :] * fade + part
            top_ref[h, 0:1, :] = best

    absorb([kv_ref], True)

    @pl.when(core == 1)
    def _():
        kv_beside().wait_recv()
        absorb([kvs.at[0]], False)

    def two(d, _):
        kv_forward(d, core).wait_recv()
        absorb([kvs.at[2 * d], kvs.at[2 * d + 1]], False)
        return 0

    lax.fori_loop(1, place + 1, two, 0)
    for h in range(heads):
        total = sum_ref[h, 0:1, :]
        own_ref[h] = (acc_ref[h] / total).T
        lse_ref[h] = jnp.broadcast_to(top_ref[h, 0:1, :] + jnp.log2(total), lse_ref.shape[1:])

    def finish(k, _):
        homeward(k, sibling).wait_recv()
        outward(k, sibling).wait_send()
        homeward(k, sibling).wait_send()
        return 0

    lax.fori_loop(1, owners, finish, 0)

    def finish_kv(d, _):
        kv_copy(d).wait_send()
        return 0

    lax.fori_loop(1, 8 - place, finish_kv, 0)

    @pl.when(core == 0)
    def _():
        kv_beside().wait_send()

    def finish_forward(d, _):
        kv_forward(d, core).wait_send()
        return 0

    lax.fori_loop(1, place + 1, finish_forward, 0)


def merge_kernel(picks_ref, slot_ref, table_ref, own_ref, own_lse_ref, ret, merged_ref):
    heads = own_ref.shape[0]
    feature = own_ref.shape[2]
    blocks, picked = picks_ref.shape[1:]
    item = own_ref.shape[1] // blocks
    block_rows = merged_ref.shape[0] // blocks
    fold = item // block_rows
    me = lax.axis_index("seq")
    z, x, core = lax.div(me, 8), lax.rem(lax.div(me, 2), 4), lax.rem(me, 2)

    def place_of(t):
        dz = lax.rem(lax.div(t, 8) - z + 4, 4)
        dx = lax.rem(lax.rem(lax.div(t, 2), 4) - x + 4, 4)
        return 2 * table_ref[dz, dx] + lax.rem(lax.rem(t, 2) - core + 2, 2)

    for h in range(heads):
        own = own_ref[h]
        lses = [own_lse_ref[h, 0:1, :]]
        for p in range(picked):
            pieces = []
            for b in range(blocks):
                at, c = place_of(picks_ref[h, b, p]), slot_ref[h, b, p]
                extra = ret[at, heads * 2 * item : heads * 2 * item + EXTRA, :]
                lse = jnp.sum(
                    extra.astype(jnp.float32)[3 * h : 3 * h + 3, :], axis=0, keepdims=True
                )
                pieces.append(jnp.where(c == 0, lse[:, 0:item], lse[:, item : 2 * item]))
            lses.append(jnp.concatenate(pieces, axis=1))
        best = functools.reduce(jnp.maximum, lses)
        shares = [jnp.exp2(x - best) for x in lses]
        whole = functools.reduce(jnp.add, shares)
        shares = [x / whole for x in shares]
        fill = [jnp.zeros_like(best)] * (8 - len(shares))
        columns = jnp.concatenate(shares + fill, axis=0).T
        for b in range(blocks):
            cut = slice(b * item, (b + 1) * item)
            mix = own[cut, :] * columns[cut, 0:1]
            for p in range(picked):
                at, c = place_of(picks_ref[h, b, p]), slot_ref[h, b, p]
                got = ret[at, pl.ds(pl.multiple_of((2 * h + c) * item, item), item), :]
                mix = mix + got.astype(jnp.float32) * columns[cut, p + 1 : p + 2]
            mix = mix.astype(jnp.bfloat16)
            for g in range(fold):
                lane = (h * fold + g) * feature
                merged_ref[b * block_rows : (b + 1) * block_rows, lane : lane + feature] = mix[
                    g * block_rows : (g + 1) * block_rows, :
                ]


def merge(picks, slots, own, lse, ret):
    table = [[0] * 4 for _ in range(4)]
    for i, pair in enumerate(CHIPS):
        for j, (dz, dx) in enumerate(pair):
            table[dz][dx] = 2 * i + j
    table = jnp.array(table, jnp.int32)
    return pl.pallas_call(
        merge_kernel,
        out_shape=jax.ShapeDtypeStruct((256, 8 * own.shape[2]), jnp.bfloat16),
        in_specs=[SM, SM, SM, VM, VM, VM],
        out_specs=VM,
        compiler_params=pltpu.CompilerParams(vmem_limit_bytes=BIG),
    )(picks, slots, table, own, lse, ret)


def exchange(outgoing, keys, values, q, kv):
    owners, heads, slot_rows, feature = outgoing.shape
    rows = q.shape[1]
    back = (owners, heads * slot_rows + EXTRA, feature)
    dma = pltpu.SemaphoreType.DMA
    return pl.pallas_call(
        exchange_kernel,
        out_shape=(
            jax.ShapeDtypeStruct(back, jnp.bfloat16),
            jax.ShapeDtypeStruct((heads, rows, feature), jnp.float32),
            jax.ShapeDtypeStruct((heads, 8, rows), jnp.float32),
        ),
        in_specs=[VM, ANY, ANY, VM, VM],
        out_specs=(VM, VM, VM),
        scratch_shapes=[
            pltpu.VMEM((2,) + keys.shape, jnp.bfloat16),
            pltpu.VMEM((heads, KB, feature), jnp.bfloat16),
            pltpu.VMEM((heads, feature, KB), jnp.bfloat16),
            pltpu.VMEM(outgoing.shape, jnp.bfloat16),
            pltpu.VMEM(back, jnp.bfloat16),
            pltpu.VMEM((16,) + kv.shape, jnp.bfloat16),
            pltpu.VMEM((heads, feature, rows), jnp.float32),
            pltpu.VMEM((heads, 8, rows), jnp.float32),
            pltpu.VMEM((heads, 8, rows), jnp.float32),
            dma((2,)),
            dma((owners,)),
            dma((owners,)),
            dma((owners,)),
            dma((owners,)),
            dma((8,)),
            dma((8,)),
            dma((8,)),
            dma((8,)),
        ],
        compiler_params=pltpu.CompilerParams(
            collective_id=0, has_side_effects=True, vmem_limit_bytes=BIG
        ),
    )(outgoing, keys, values, q, kv)


def project_kernel(
    m_ref, w_ref, out_ref, w_buf, order, sent1, keep, got1, sent2, mine2, got2,
    load_sem, send1, recv1, send2, recv2,
):
    parts, depth, wide = w_buf.shape
    y = lax.axis_index("kvh")
    beside = y + 1 - 2 * lax.rem(y, 2)
    across = 3 - y
    far = 3 - beside
    rows = m_ref.shape[0] // 4

    loads = [
        pltpu.make_async_copy(w_ref.at[:, n * wide : (n + 1) * wide], w_buf.at[n], load_sem.at[n])
        for n in range(parts)
    ]
    for load in loads:
        load.start()
    barrier = pltpu.get_barrier_semaphore()
    for other in (beside, across):
        pl.semaphore_signal(barrier, inc=1, device_id={"kvh": other}, device_id_type=MESH)
    for kind, blocks in enumerate(((beside, far, across, y), (across, far, beside, y))):
        for i, b in enumerate(blocks):
            order[kind, i * rows : (i + 1) * rows, :] = m_ref[
                pl.ds(pl.multiple_of(b * rows, rows), rows), :
            ]
    pl.semaphore_wait(barrier, 2)

    def first_copy(n):
        return pltpu.make_async_remote_copy(
            src_ref=sent1.at[n],
            dst_ref=got1.at[n],
            send_sem=send1.at[n],
            recv_sem=recv1.at[n],
            device_id={"kvh": beside if n % 2 == 0 else across},
            device_id_type=MESH,
        )

    def second_copy(n):
        return pltpu.make_async_remote_copy(
            src_ref=sent2.at[n],
            dst_ref=got2.at[n],
            send_sem=send2.at[n],
            recv_sem=recv2.at[n],
            device_id={"kvh": across if n % 2 == 0 else beside},
            device_id_type=MESH,
        )

    def forward(n):
        first_copy(n).wait_recv()
        both = got1[n].astype(jnp.float32)
        sent2[n] = (keep[n, 0:rows, :] + both[rows:, :]).astype(jnp.bfloat16)
        mine2[n] = keep[n, rows:, :] + both[0:rows, :]
        second_copy(n).start()

    for n in range(parts):
        loads[n].wait()
        product = jnp.dot(order[n % 2], w_buf[n], preferred_element_type=jnp.float32)
        sent1[n] = product[0 : 2 * rows, :].astype(jnp.bfloat16)
        keep[n] = product[2 * rows :, :]
        first_copy(n).start()
        if n >= LAG:
            forward(n - LAG)
    for n in range(parts - LAG, parts):
        forward(n)
    for n in range(parts):
        second_copy(n).wait_recv()
        out_ref[:, n * wide : (n + 1) * wide] = (
            mine2[n] + got2[n].astype(jnp.float32)
        ).astype(jnp.bfloat16)
    for n in range(parts):
        first_copy(n).wait_send()
        second_copy(n).wait_send()


def project(merged, weight):
    rows, depth = merged.shape
    width = weight.shape[1]
    parts = 8
    wide = width // parts
    quarter = rows // 4
    dma = pltpu.SemaphoreType.DMA
    return pl.pallas_call(
        project_kernel,
        out_shape=jax.ShapeDtypeStruct((quarter, width), jnp.bfloat16),
        in_specs=[VM, ANY],
        out_specs=VM,
        scratch_shapes=[
            pltpu.VMEM((parts, depth, wide), jnp.bfloat16),
            pltpu.VMEM((2, rows, depth), jnp.bfloat16),
            pltpu.VMEM((parts, 2 * quarter, wide), jnp.bfloat16),
            pltpu.VMEM((parts, 2 * quarter, wide), jnp.float32),
            pltpu.VMEM((parts, 2 * quarter, wide), jnp.bfloat16),
            pltpu.VMEM((parts, quarter, wide), jnp.bfloat16),
            pltpu.VMEM((parts, quarter, wide), jnp.float32),
            pltpu.VMEM((parts, quarter, wide), jnp.bfloat16),
            dma((parts,)),
            dma((parts,)),
            dma((parts,)),
            dma((parts,)),
            dma((parts,)),
        ],
        compiler_params=pltpu.CompilerParams(
            collective_id=1, has_side_effects=True, vmem_limit_bytes=BIG
        ),
    )(merged, weight)


def on_device(queries, ctx_keys, ctx_values, new_keys, new_values, picks, out_weight):
    q = queries.reshape(16, 16, 2, 4, 128).transpose(2, 0, 3, 1, 4).reshape(2, 1024, 128)
    outgoing, slots = place(picks, q)
    keys = ctx_keys.reshape(8192, 128)
    values = ctx_values.reshape(8192, 128)
    new_t = new_values.reshape(2, 128, 2, 128).transpose(2, 0, 3, 1).reshape(2, 256, 128)
    kv = jnp.stack([new_keys.transpose(1, 0, 2), new_t])
    ret, own, lse = exchange(outgoing, keys, values, q, kv)
    merged = merge(picks, slots, own, lse, ret)
    return project(merged, out_weight)


def solution(mesh):
    placed = (
        P("seq", "kvh", None),
        P("seq", "kvh", None),
        P("seq", "kvh", None),
        P("seq", "kvh", None),
        P("seq", "kvh", None),
        P("kvh", "seq", None),
        P("kvh", None),
    )
    return jax.shard_map(
        on_device, mesh=mesh, in_specs=placed, out_specs=P(("seq", "kvh"), None), check_vma=False
    )
```

```python
import functools

import jax
import jax.numpy as jnp
from jax import lax
from jax.experimental import pallas as pl
from jax.experimental.pallas import tpu as pltpu
from jax.sharding import PartitionSpec as P

LOG2E = 1.4426950408889634
NT = (((1,), (1,)), ((), ()))
TN = (((0,), (0,)), ((), ()))
VM = pl.BlockSpec(memory_space=pltpu.VMEM)
SM = pl.BlockSpec(memory_space=pltpu.SMEM)
KB = 4096
BIG = 60 * 2**20
EXTRA = 16
LAG = 3
SPREAD_AT = 3
MESH = pl.DeviceIdType.MESH
ANY = pl.BlockSpec(memory_space=pl.ANY)


def split_queries(rows):
    scale = LOG2E * float(rows.shape[-1]) ** -0.5
    scaled = rows.astype(jnp.float32) * scale
    high = scaled.astype(jnp.bfloat16)
    low = (scaled - high.astype(jnp.float32)).astype(jnp.bfloat16)
    return jnp.concatenate([high, low], axis=1)


def scores_of(keys, split):
    return lax.dot_general(
        jnp.concatenate([keys, keys], axis=1), split, NT, preferred_element_type=jnp.float32
    )


def attend_tile(rows, keys_at, values_t_at, chunks):
    split = split_queries(rows)
    top = total = acc = None
    now = scores_of(keys_at(0), split)
    for c in range(chunks):
        later = scores_of(keys_at(c + 1), split) if c + 1 < chunks else None
        best = jnp.max(now, axis=0, keepdims=True)
        best = best if top is None else jnp.maximum(top, best)
        e = jnp.exp2(now - best)
        part = jnp.sum(e, axis=0, keepdims=True)
        out = jnp.dot(values_t_at(c), e.astype(jnp.bfloat16), preferred_element_type=jnp.float32)
        if top is None:
            acc, total = out, part
        else:
            fade = jnp.exp2(top - best)
            acc, total = acc * fade + out, total * fade + part
        top, now = best, later
    return acc / total, top + jnp.log2(total)


def three_parts(rows):
    parts = []
    for row in rows:
        high = row.astype(jnp.bfloat16).astype(jnp.float32)
        rest = row - high
        mid = rest.astype(jnp.bfloat16).astype(jnp.float32)
        parts += [high, mid, rest - mid]
    fill = jnp.zeros((EXTRA - len(parts), rows[0].shape[1]), jnp.float32)
    return jnp.concatenate(parts + [fill], axis=0).astype(jnp.bfloat16)


CHIPS = (
    ((0, 0), (0, 1)), ((1, 0), (0, 3)), ((3, 0), (1, 1)), ((3, 3), (1, 3)),
    ((3, 1), (0, 2)), ((2, 0), (1, 2)), ((2, 1), (3, 2)), ((2, 3), (2, 2)),
)
DIGITS = tuple(
    sum(pair[a][b] * 4**i for i, pair in enumerate(CHIPS)) for a in range(2) for b in range(2)
)


def offsets_of(digits):
    za, xa, zb, xb = [lax.rem(x, 4) for x in digits]
    return ((za, xa, 0), (za, xa, 1), (zb, xb, 0), (zb, xb, 1))


def next_digits(digits):
    return tuple(lax.div(x, 4) for x in digits)


def first_digits():
    return tuple(jnp.int32(x) for x in DIGITS)


def place_kernel(picks_ref, raw_ref, out_ref, slot_ref, q_ref, count_ref):
    heads, blocks, picked = picks_ref.shape
    item = q_ref.shape[1] // blocks
    both = heads * item
    streams = both // 16
    to = lax.broadcasted_iota(jnp.int32, (both, both), 0)
    frm = lax.broadcasted_iota(jnp.int32, (both, both), 1)
    picking = (frm == lax.rem(to, 16) * streams + lax.div(to, 16)).astype(jnp.bfloat16)
    for b in range(blocks):
        rows = jnp.dot(
            picking, raw_ref[b * both : (b + 1) * both, :], preferred_element_type=jnp.float32
        ).astype(jnp.bfloat16)
        for h in range(heads):
            q_ref[h, b * item : (b + 1) * item, :] = rows[h * item : (h + 1) * item, :]
    owners = out_ref.shape[0]
    out_ref[...] = jnp.zeros_like(out_ref)

    def clear(i, _):
        for h in range(heads):
            count_ref[h, i] = 0
        return 0

    lax.fori_loop(0, owners, clear, 0)
    for h in range(heads):

        def one(q, _):
            rows = q_ref[h, pl.ds(pl.multiple_of(q * item, item), item), :]
            for p in range(picked):
                t = picks_ref[h, q, p]
                c = count_ref[h, t]
                count_ref[h, t] = c + 1
                slot_ref[h, q, p] = c
                out_ref[t, h, pl.ds(pl.multiple_of(c * item, item), item), :] = rows
            return 0

        lax.fori_loop(0, blocks, one, 0)


def place(picks, raw):
    heads, blocks, picked = picks.shape
    feature = raw.shape[1]
    rows = raw.shape[0] // heads
    return pl.pallas_call(
        place_kernel,
        out_shape=(
            jax.ShapeDtypeStruct((32, heads, 128, feature), jnp.bfloat16),
            jax.ShapeDtypeStruct(picks.shape, jnp.int32),
            jax.ShapeDtypeStruct((heads, rows, feature), jnp.bfloat16),
        ),
        in_specs=[SM, VM],
        out_specs=(VM, SM, VM),
        scratch_shapes=[pltpu.SMEM((heads, 32), jnp.int32)],
        compiler_params=pltpu.CompilerParams(vmem_limit_bytes=BIG),
    )(picks, raw)


def exchange_kernel(
    out_ref, key_ref, value_ref, q_ref, new_key_ref, new_value_ref, ret, own_ref, lse_ref,
    kv_ref, raw, keys, values, arrived, done, kvs, acc_ref, top_ref, sum_ref,
    load_sem, send_sem, recv_sem, back_sem, home_sem, kv_send, kv_recv, fwd_send, fwd_recv, spread_send,
):
    owners, heads, slot_rows, feature = out_ref.shape
    me = lax.axis_index("seq")
    z, x, core = lax.div(me, 8), lax.rem(lax.div(me, 2), 4), lax.rem(me, 2)
    sibling = me + 1 - 2 * core
    lower = lax.rem(z, 2)
    place = lower * 4 + x
    sent_until = (1 - core) * (8 - place) + core * (4 - x)
    group, step = 4, 1024

    loads = [
        pltpu.make_async_copy(key_ref, raw.at[0], load_sem.at[0]),
        pltpu.make_async_copy(value_ref, raw.at[1], load_sem.at[1]),
    ]
    for load in loads:
        load.start()
    barrier = pltpu.get_barrier_semaphore()

    def greet(d, _):
        pl.semaphore_signal(
            barrier, inc=1, device_id={"seq": lax.rem(me + d, owners)}, device_id_type=MESH
        )
        return 0

    lax.fori_loop(1, owners, greet, 0)

    def ahead(offset):
        dz, dx, dc = offset
        return lax.rem(z + dz, 4) * 8 + lax.rem(x + dx, 4) * 2 + lax.rem(core + dc, 2)

    def behind(offset):
        dz, dx, dc = offset
        return lax.rem(z + 4 - dz, 4) * 8 + lax.rem(x + 4 - dx, 4) * 2 + lax.rem(core + dc, 2)

    def outward(k, to):
        return pltpu.make_async_remote_copy(
            src_ref=out_ref.at[to],
            dst_ref=arrived.at[k],
            send_sem=send_sem.at[k],
            recv_sem=recv_sem.at[k],
            device_id={"seq": to},
            device_id_type=MESH,
        )

    def homeward(k, to):
        return pltpu.make_async_remote_copy(
            src_ref=done.at[k],
            dst_ref=ret.at[k],
            send_sem=back_sem.at[k],
            recv_sem=home_sem.at[k],
            device_id={"seq": to},
            device_id_type=MESH,
        )

    def kv_copy(d):
        return pltpu.make_async_remote_copy(
            src_ref=kv_ref,
            dst_ref=kvs.at[2 * d + core],
            send_sem=kv_send.at[d],
            recv_sem=kv_recv.at[d],
            device_id={"seq": lax.rem(me + 2 * d, owners)},
            device_id_type=MESH,
        )

    def kv_spread(o):
        other = lax.rem(x + o, 4)
        return pltpu.make_async_remote_copy(
            src_ref=kvs.at[9],
            dst_ref=kvs.at[2 * (4 + other - x) + 1],
            send_sem=spread_send.at[o],
            recv_sem=kv_recv.at[4 + other - x],
            device_id={"seq": z * 8 + other * 2 + 1},
            device_id_type=MESH,
        )

    def kv_beside():
        return pltpu.make_async_remote_copy(
            src_ref=kv_ref,
            dst_ref=kvs.at[0],
            send_sem=kv_send.at[0],
            recv_sem=kv_recv.at[0],
            device_id={"seq": sibling},
            device_id_type=MESH,
        )

    def kv_forward(d, from_core):
        return pltpu.make_async_remote_copy(
            src_ref=kvs.at[2 * d + from_core],
            dst_ref=kvs.at[2 * d + from_core],
            send_sem=fwd_send.at[d],
            recv_sem=fwd_recv.at[d],
            device_id={"seq": sibling},
            device_id_type=MESH,
        )

    span = 2 * feature
    row = lax.broadcasted_iota(jnp.int32, (span, span), 0)
    col = lax.broadcasted_iota(jnp.int32, (span, span), 1)
    picking = (col == 2 * lax.rem(row, feature) + lax.div(row, feature)).astype(jnp.bfloat16)
    placing = (row == 2 * lax.rem(col, feature) + lax.div(col, feature)).astype(jnp.bfloat16)

    for j in range(new_key_ref.shape[0] // span):
        cut = slice(j * feature, (j + 1) * feature)
        block = new_key_ref[j * span : (j + 1) * span, :]
        both = jnp.dot(picking, block, preferred_element_type=jnp.float32).astype(jnp.bfloat16)
        for h in range(heads):
            kv_ref[0, h, cut, :] = both[h * feature : (h + 1) * feature, :]
        block = new_value_ref[j * span : (j + 1) * span, :]
        both = lax.dot_general(block, placing, TN, preferred_element_type=jnp.float32)
        both = both.astype(jnp.bfloat16)
        for h in range(heads):
            kv_ref[1, h, cut, :] = both[:, h * feature : (h + 1) * feature]

    pl.semaphore_wait(barrier, owners - 1)

    def start_out(i, digits):
        for j, offset in enumerate(offsets_of(digits)):
            k = i * group + j
            if j == 0:

                @pl.when(i > 0)
                def _():
                    outward(k, ahead(offset)).start()

            else:
                outward(k, ahead(offset)).start()
        return next_digits(digits)

    lax.fori_loop(0, owners // group, start_out, first_digits())

    def start_kv(d, _):
        kv_copy(d).start()
        return 0

    lax.fori_loop(1, sent_until, start_kv, 0)

    @pl.when((1 - lower) * core == 1)
    def _():
        kv_copy(4).start()

    @pl.when(core == 0)
    def _():
        kv_beside().start()

    arrived[0] = out_ref[me]
    loads[0].wait()

    def sort_keys(j, _):
        block = raw[0, pl.ds(pl.multiple_of(j * span, span), span), :]
        both = jnp.dot(picking, block, preferred_element_type=jnp.float32).astype(jnp.bfloat16)
        for h in range(heads):
            keys[h, pl.ds(pl.multiple_of(j * feature, feature), feature), :] = both[
                h * feature : (h + 1) * feature, :
            ]
        return 0

    lax.fori_loop(0, KB // feature, sort_keys, 0, unroll=4)
    loads[1].wait()

    def sort_values(j, _):
        block = raw[1, pl.ds(pl.multiple_of(j * span, span), span), :]
        both = lax.dot_general(block, placing, TN, preferred_element_type=jnp.float32)
        both = both.astype(jnp.bfloat16)
        for h in range(heads):
            values[h, :, pl.ds(pl.multiple_of(j * feature, feature), feature)] = both[
                :, h * feature : (h + 1) * feature
            ]
        return 0

    lax.fori_loop(0, KB // feature, sort_values, 0, unroll=4)

    spreads = lower * core

    def tile(i, digits):
        first = i * group

        @pl.when(spreads * lax.div(i + 8 - SPREAD_AT, 8) * lax.div(8 + SPREAD_AT - i, 8) == 1)
        def _():
            kv_copy(4).wait_recv()
            for o in range(1, 4):
                kv_spread(o).start()

        offsets = offsets_of(digits)
        for j, offset in enumerate(offsets):
            if j == 0:

                @pl.when(i > 0)
                def _():
                    outward(first, sibling).wait_recv()

            else:
                outward(first + j, sibling).wait_recv()
        lses = []
        for h in range(heads):
            rows = jnp.concatenate([arrived[first + j, h] for j in range(group)], axis=0)
            out, lse = attend_tile(
                rows,
                lambda c: keys[h, c * step : (c + 1) * step, :],
                lambda c: values[h, :, c * step : (c + 1) * step],
                KB // step,
            )
            out = out.T.astype(jnp.bfloat16)
            lses.append(lse)
            for j in range(group):
                cut = slice(j * slot_rows, (j + 1) * slot_rows)
                done[first + j, h * slot_rows : (h + 1) * slot_rows, :] = out[cut, :]
        for j, offset in enumerate(offsets):
            cut = slice(j * slot_rows, (j + 1) * slot_rows)
            done[first + j, heads * slot_rows : heads * slot_rows + EXTRA, :] = three_parts(
                [lse[:, cut] for lse in lses]
            )
            if j == 0:

                @pl.when(i > 0)
                def _():
                    homeward(first, behind(offset)).start()

            else:
                homeward(first + j, behind(offset)).start()
        return next_digits(digits)

    lax.fori_loop(0, owners // group, tile, first_digits())
    ret[0] = done[0]

    item = slot_rows // 2
    block_rows = item // 4
    half = kv_ref.shape[2] // 2

    def pass_on(d, _):
        @pl.when(jnp.logical_or(d != 4, spreads == 0))
        def _():
            kv_copy(d).wait_recv()

        kv_forward(d, core).start()
        return 0

    lax.fori_loop(1, place + 1, pass_on, 0)

    def absorb(pairs, first):
        for h in range(heads):
            split = split_queries(q_ref[h])
            key_rows = [ref[0, h] for ref in pairs]
            key_rows = key_rows[0] if len(pairs) == 1 else jnp.concatenate(key_rows, axis=0)
            value_t = jnp.concatenate(
                [ref[1, h, at : at + half, :] for ref in pairs for at in (0, half)], axis=1
            )
            s = scores_of(key_rows, split)
            if first:
                key_at = lax.broadcasted_iota(jnp.int32, s.shape, 0)
                lane = lax.broadcasted_iota(jnp.int32, s.shape, 1)
                row_at = (lane // item) * block_rows + lax.rem(lane, block_rows)
                s = jnp.where(key_at <= row_at, s, -1e30)
            best = jnp.max(s, axis=0, keepdims=True)
            if not first:
                best = jnp.maximum(top_ref[h, 0:1, :], best)
            e = jnp.exp2(s - best)
            part = jnp.sum(e, axis=0, keepdims=True)
            o = jnp.dot(value_t, e.astype(jnp.bfloat16), preferred_element_type=jnp.float32)
            if first:
                acc_ref[h] = o
                sum_ref[h, 0:1, :] = part
            else:
                fade = jnp.exp2(top_ref[h, 0:1, :] - best)
                acc_ref[h] = acc_ref[h] * fade + o
                sum_ref[h, 0:1, :] = sum_ref[h, 0:1, :] * fade + part
            top_ref[h, 0:1, :] = best

    absorb([kv_ref], True)

    @pl.when(core == 1)
    def _():
        kv_beside().wait_recv()
        absorb([kvs.at[0]], False)

    def two(d, _):
        kv_forward(d, core).wait_recv()
        absorb([kvs.at[2 * d], kvs.at[2 * d + 1]], False)
        return 0

    lax.fori_loop(1, place + 1, two, 0)
    for h in range(heads):
        total = sum_ref[h, 0:1, :]
        own_ref[h] = (acc_ref[h] / total).T
        lse_ref[h] = jnp.broadcast_to(top_ref[h, 0:1, :] + jnp.log2(total), lse_ref.shape[1:])

    def finish(k, _):
        homeward(k, sibling).wait_recv()
        outward(k, sibling).wait_send()
        homeward(k, sibling).wait_send()
        return 0

    lax.fori_loop(1, owners, finish, 0)

    def finish_kv(d, _):
        kv_copy(d).wait_send()
        return 0

    lax.fori_loop(1, sent_until, finish_kv, 0)

    @pl.when((1 - lower) * core == 1)
    def _():
        kv_copy(4).wait_send()

    @pl.when(spreads == 1)
    def _():
        for o in range(1, 4):
            kv_spread(o).wait_send()

    @pl.when(core == 0)
    def _():
        kv_beside().wait_send()

    def finish_forward(d, _):
        kv_forward(d, core).wait_send()
        return 0

    lax.fori_loop(1, place + 1, finish_forward, 0)


def merge_kernel(picks_ref, slot_ref, table_ref, own_ref, own_lse_ref, ret, merged_ref):
    heads = own_ref.shape[0]
    feature = own_ref.shape[2]
    blocks, picked = picks_ref.shape[1:]
    item = own_ref.shape[1] // blocks
    block_rows = merged_ref.shape[0] // blocks
    fold = item // block_rows
    me = lax.axis_index("seq")
    z, x, core = lax.div(me, 8), lax.rem(lax.div(me, 2), 4), lax.rem(me, 2)

    def place_of(t):
        dz = lax.rem(lax.div(t, 8) - z + 4, 4)
        dx = lax.rem(lax.rem(lax.div(t, 2), 4) - x + 4, 4)
        return 2 * table_ref[dz, dx] + lax.rem(lax.rem(t, 2) - core + 2, 2)

    for h in range(heads):
        own = own_ref[h]
        lses = [own_lse_ref[h, 0:1, :]]
        for p in range(picked):
            pieces = []
            for b in range(blocks):
                at, c = place_of(picks_ref[h, b, p]), slot_ref[h, b, p]
                extra = ret[at, heads * 2 * item : heads * 2 * item + EXTRA, :]
                lse = jnp.sum(
                    extra.astype(jnp.float32)[3 * h : 3 * h + 3, :], axis=0, keepdims=True
                )
                pieces.append(jnp.where(c == 0, lse[:, 0:item], lse[:, item : 2 * item]))
            lses.append(jnp.concatenate(pieces, axis=1))
        best = functools.reduce(jnp.maximum, lses)
        shares = [jnp.exp2(x - best) for x in lses]
        whole = functools.reduce(jnp.add, shares)
        shares = [x / whole for x in shares]
        fill = [jnp.zeros_like(best)] * (8 - len(shares))
        columns = jnp.concatenate(shares + fill, axis=0).T
        for b in range(blocks):
            cut = slice(b * item, (b + 1) * item)
            mix = own[cut, :] * columns[cut, 0:1]
            for p in range(picked):
                at, c = place_of(picks_ref[h, b, p]), slot_ref[h, b, p]
                got = ret[at, pl.ds(pl.multiple_of((2 * h + c) * item, item), item), :]
                mix = mix + got.astype(jnp.float32) * columns[cut, p + 1 : p + 2]
            mix = mix.astype(jnp.bfloat16)
            for g in range(fold):
                lane = (h * fold + g) * feature
                merged_ref[b * block_rows : (b + 1) * block_rows, lane : lane + feature] = mix[
                    g * block_rows : (g + 1) * block_rows, :
                ]


def merge(picks, slots, own, lse, ret):
    table = [[0] * 4 for _ in range(4)]
    for i, pair in enumerate(CHIPS):
        for j, (dz, dx) in enumerate(pair):
            table[dz][dx] = 2 * i + j
    table = jnp.array(table, jnp.int32)
    return pl.pallas_call(
        merge_kernel,
        out_shape=jax.ShapeDtypeStruct((256, 8 * own.shape[2]), jnp.bfloat16),
        in_specs=[SM, SM, SM, VM, VM, VM],
        out_specs=VM,
        compiler_params=pltpu.CompilerParams(vmem_limit_bytes=BIG),
    )(picks, slots, table, own, lse, ret)


def exchange(outgoing, keys, values, q, new_keys, new_values):
    owners, heads, slot_rows, feature = outgoing.shape
    rows = q.shape[1]
    kv_shape = (2, heads, new_keys.shape[0] // heads, feature)
    back = (owners, heads * slot_rows + EXTRA, feature)
    dma = pltpu.SemaphoreType.DMA
    return pl.pallas_call(
        exchange_kernel,
        out_shape=(
            jax.ShapeDtypeStruct(back, jnp.bfloat16),
            jax.ShapeDtypeStruct((heads, rows, feature), jnp.float32),
            jax.ShapeDtypeStruct((heads, 8, rows), jnp.float32),
        ),
        in_specs=[VM, ANY, ANY, VM, VM, VM],
        out_specs=(VM, VM, VM),
        scratch_shapes=[
            pltpu.VMEM(kv_shape, jnp.bfloat16),
            pltpu.VMEM((2,) + keys.shape, jnp.bfloat16),
            pltpu.VMEM((heads, KB, feature), jnp.bfloat16),
            pltpu.VMEM((heads, feature, KB), jnp.bfloat16),
            pltpu.VMEM(outgoing.shape, jnp.bfloat16),
            pltpu.VMEM(back, jnp.bfloat16),
            pltpu.VMEM((16,) + kv_shape, jnp.bfloat16),
            pltpu.VMEM((heads, feature, rows), jnp.float32),
            pltpu.VMEM((heads, 8, rows), jnp.float32),
            pltpu.VMEM((heads, 8, rows), jnp.float32),
            dma((2,)),
            dma((owners,)),
            dma((owners,)),
            dma((owners,)),
            dma((owners,)),
            dma((8,)),
            dma((8,)),
            dma((8,)),
            dma((8,)),
            dma((4,)),
        ],
        compiler_params=pltpu.CompilerParams(
            collective_id=0, has_side_effects=True, vmem_limit_bytes=BIG
        ),
    )(outgoing, keys, values, q, new_keys, new_values)


def project_kernel(
    m_ref, w_ref, out_ref, w_buf, order, sent1, keep, got1, sent2, mine2, got2,
    load_sem, send1, recv1, send2, recv2,
):
    parts, depth, wide = w_buf.shape
    y = lax.axis_index("kvh")
    beside = y + 1 - 2 * lax.rem(y, 2)
    across = 3 - y
    far = 3 - beside
    rows = m_ref.shape[0] // 4

    loads = [
        pltpu.make_async_copy(w_ref.at[:, n * wide : (n + 1) * wide], w_buf.at[n], load_sem.at[n])
        for n in range(parts)
    ]
    for load in loads:
        load.start()
    barrier = pltpu.get_barrier_semaphore()
    for other in (beside, across):
        pl.semaphore_signal(barrier, inc=1, device_id={"kvh": other}, device_id_type=MESH)
    for kind, blocks in enumerate(((beside, far, across, y), (across, far, beside, y))):
        for i, b in enumerate(blocks):
            order[kind, i * rows : (i + 1) * rows, :] = m_ref[
                pl.ds(pl.multiple_of(b * rows, rows), rows), :
            ]
    pl.semaphore_wait(barrier, 2)

    def first_copy(n):
        return pltpu.make_async_remote_copy(
            src_ref=sent1.at[n],
            dst_ref=got1.at[n],
            send_sem=send1.at[n],
            recv_sem=recv1.at[n],
            device_id={"kvh": beside if n % 2 == 0 else across},
            device_id_type=MESH,
        )

    def second_copy(n):
        return pltpu.make_async_remote_copy(
            src_ref=sent2.at[n],
            dst_ref=got2.at[n],
            send_sem=send2.at[n],
            recv_sem=recv2.at[n],
            device_id={"kvh": across if n % 2 == 0 else beside},
            device_id_type=MESH,
        )

    def forward(n):
        first_copy(n).wait_recv()
        both = got1[n].astype(jnp.float32)
        sent2[n] = (keep[n, 0:rows, :] + both[rows:, :]).astype(jnp.bfloat16)
        mine2[n] = keep[n, rows:, :] + both[0:rows, :]
        second_copy(n).start()

    for n in range(parts):
        loads[n].wait()
        product = jnp.dot(order[n % 2], w_buf[n], preferred_element_type=jnp.float32)
        sent1[n] = product[0 : 2 * rows, :].astype(jnp.bfloat16)
        keep[n] = product[2 * rows :, :]
        first_copy(n).start()
        if n >= LAG:
            forward(n - LAG)
    for n in range(parts - LAG, parts):
        forward(n)
    for n in range(parts):
        second_copy(n).wait_recv()
        out_ref[:, n * wide : (n + 1) * wide] = (
            mine2[n] + got2[n].astype(jnp.float32)
        ).astype(jnp.bfloat16)
    for n in range(parts):
        first_copy(n).wait_send()
        second_copy(n).wait_send()


def project(merged, weight):
    rows, depth = merged.shape
    width = weight.shape[1]
    parts = 16
    wide = width // parts
    quarter = rows // 4
    dma = pltpu.SemaphoreType.DMA
    return pl.pallas_call(
        project_kernel,
        out_shape=jax.ShapeDtypeStruct((quarter, width), jnp.bfloat16),
        in_specs=[VM, ANY],
        out_specs=VM,
        scratch_shapes=[
            pltpu.VMEM((parts, depth, wide), jnp.bfloat16),
            pltpu.VMEM((2, rows, depth), jnp.bfloat16),
            pltpu.VMEM((parts, 2 * quarter, wide), jnp.bfloat16),
            pltpu.VMEM((parts, 2 * quarter, wide), jnp.float32),
            pltpu.VMEM((parts, 2 * quarter, wide), jnp.bfloat16),
            pltpu.VMEM((parts, quarter, wide), jnp.bfloat16),
            pltpu.VMEM((parts, quarter, wide), jnp.float32),
            pltpu.VMEM((parts, quarter, wide), jnp.bfloat16),
            dma((parts,)),
            dma((parts,)),
            dma((parts,)),
            dma((parts,)),
            dma((parts,)),
        ],
        compiler_params=pltpu.CompilerParams(
            collective_id=1, has_side_effects=True, vmem_limit_bytes=BIG
        ),
    )(merged, weight)


def on_device(queries, ctx_keys, ctx_values, new_keys, new_values, picks, out_weight):
    outgoing, slots, q = place(picks, queries.reshape(2048, 128))
    flat = [x.reshape(-1, 128) for x in (ctx_keys, ctx_values, new_keys, new_values)]
    ret, own, lse = exchange(outgoing, flat[0], flat[1], q, flat[2], flat[3])
    merged = merge(picks, slots, own, lse, ret)
    return project(merged, out_weight)


def solution(mesh):
    placed = (
        P("seq", "kvh", None),
        P("seq", "kvh", None),
        P("seq", "kvh", None),
        P("seq", "kvh", None),
        P("seq", "kvh", None),
        P("kvh", "seq", None),
        P("kvh", None),
    )
    return jax.shard_map(
        on_device, mesh=mesh, in_specs=placed, out_specs=P(("seq", "kvh"), None), check_vma=False
    )
```

```python
import functools

import jax
import jax.numpy as jnp
from jax import lax
from jax.experimental import pallas as pl
from jax.experimental.pallas import tpu as pltpu
from jax.sharding import PartitionSpec as P

LOG2E = 1.4426950408889634
NT = (((1,), (1,)), ((), ()))
TN = (((0,), (0,)), ((), ()))
VM = pl.BlockSpec(memory_space=pltpu.VMEM)
SM = pl.BlockSpec(memory_space=pltpu.SMEM)
KB = 4096
BIG = 60 * 2**20
EXTRA = 16
LAG = 3
EARLY = 2
SPREAD_AT = 2
OWN_AT = 5
MESH = pl.DeviceIdType.MESH
ANY = pl.BlockSpec(memory_space=pl.ANY)


def split_queries(rows):
    scale = LOG2E * float(rows.shape[-1]) ** -0.5
    scaled = rows.astype(jnp.float32) * scale
    high = scaled.astype(jnp.bfloat16)
    low = (scaled - high.astype(jnp.float32)).astype(jnp.bfloat16)
    return jnp.concatenate([high, low], axis=1)


def scores_of(keys, split):
    return lax.dot_general(
        jnp.concatenate([keys, keys], axis=1), split, NT, preferred_element_type=jnp.float32
    )


def attend_tile(rows, keys_at, values_t_at, chunks):
    split = split_queries(rows)
    top = total = acc = None
    now = scores_of(keys_at(0), split)
    for c in range(chunks):
        later = scores_of(keys_at(c + 1), split) if c + 1 < chunks else None
        best = jnp.max(now, axis=0, keepdims=True)
        best = best if top is None else jnp.maximum(top, best)
        e = jnp.exp2(now - best)
        part = jnp.sum(e, axis=0, keepdims=True)
        out = jnp.dot(values_t_at(c), e.astype(jnp.bfloat16), preferred_element_type=jnp.float32)
        if top is None:
            acc, total = out, part
        else:
            fade = jnp.exp2(top - best)
            acc, total = acc * fade + out, total * fade + part
        top, now = best, later
    return acc / total, top + jnp.log2(total)


def three_parts(rows):
    parts = []
    for row in rows:
        high = row.astype(jnp.bfloat16).astype(jnp.float32)
        rest = row - high
        mid = rest.astype(jnp.bfloat16).astype(jnp.float32)
        parts += [high, mid, rest - mid]
    fill = jnp.zeros((EXTRA - len(parts), rows[0].shape[1]), jnp.float32)
    return jnp.concatenate(parts + [fill], axis=0).astype(jnp.bfloat16)


CHIPS = (
    ((0, 0), (0, 1)), ((1, 0), (0, 3)), ((3, 0), (1, 1)), ((3, 3), (1, 3)),
    ((3, 1), (0, 2)), ((2, 0), (1, 2)), ((2, 1), (3, 2)), ((2, 3), (2, 2)),
)
DIGITS = tuple(
    sum(pair[a][b] * 4**i for i, pair in enumerate(CHIPS)) for a in range(2) for b in range(2)
)


def offsets_of(digits):
    za, xa, zb, xb = [lax.rem(x, 4) for x in digits]
    return ((za, xa, 0), (za, xa, 1), (zb, xb, 0), (zb, xb, 1))


def next_digits(digits):
    return tuple(lax.div(x, 4) for x in digits)


def first_digits():
    return tuple(jnp.int32(x) for x in DIGITS)


def place_kernel(picks_ref, raw_ref, out_ref, slot_ref, q_ref, count_ref):
    heads, blocks, picked = picks_ref.shape
    item = q_ref.shape[1] // blocks
    both = heads * item
    streams = both // 16
    to = lax.broadcasted_iota(jnp.int32, (both, both), 0)
    frm = lax.broadcasted_iota(jnp.int32, (both, both), 1)
    picking = (frm == lax.rem(to, 16) * streams + lax.div(to, 16)).astype(jnp.bfloat16)
    for b in range(blocks):
        rows = jnp.dot(
            picking, raw_ref[b * both : (b + 1) * both, :], preferred_element_type=jnp.float32
        ).astype(jnp.bfloat16)
        for h in range(heads):
            q_ref[h, b * item : (b + 1) * item, :] = rows[h * item : (h + 1) * item, :]
    owners = out_ref.shape[0]
    out_ref[...] = jnp.zeros_like(out_ref)

    def clear(i, _):
        for h in range(heads):
            count_ref[h, i] = 0
        return 0

    lax.fori_loop(0, owners, clear, 0)
    for h in range(heads):

        def one(q, _):
            rows = q_ref[h, pl.ds(pl.multiple_of(q * item, item), item), :]
            for p in range(picked):
                t = picks_ref[h, q, p]
                c = count_ref[h, t]
                count_ref[h, t] = c + 1
                slot_ref[h, q, p] = c
                out_ref[t, h, pl.ds(pl.multiple_of(c * item, item), item), :] = rows
            return 0

        lax.fori_loop(0, blocks, one, 0)


def place(picks, raw):
    heads, blocks, picked = picks.shape
    feature = raw.shape[1]
    rows = raw.shape[0] // heads
    return pl.pallas_call(
        place_kernel,
        out_shape=(
            jax.ShapeDtypeStruct((32, heads, 128, feature), jnp.bfloat16),
            jax.ShapeDtypeStruct(picks.shape, jnp.int32),
            jax.ShapeDtypeStruct((heads, rows, feature), jnp.bfloat16),
        ),
        in_specs=[SM, VM],
        out_specs=(VM, SM, VM),
        scratch_shapes=[pltpu.SMEM((heads, 32), jnp.int32)],
        compiler_params=pltpu.CompilerParams(vmem_limit_bytes=BIG),
    )(picks, raw)


def exchange_kernel(
    out_ref, key_ref, value_ref, q_ref, new_key_ref, new_value_ref, ret, own_ref, lse_ref,
    kv_ref, raw, keys, values, arrived, done, kvs, acc_ref, top_ref, sum_ref,
    load_sem, send_sem, recv_sem, back_sem, home_sem, kv_send, kv_recv, fwd_send, fwd_recv, spread_send,
):
    owners, heads, slot_rows, feature = out_ref.shape
    me = lax.axis_index("seq")
    z, x, core = lax.div(me, 8), lax.rem(lax.div(me, 2), 4), lax.rem(me, 2)
    sibling = me + 1 - 2 * core
    lower = lax.rem(z, 2)
    place = lower * 4 + x
    sent_until = (1 - core) * (8 - place) + core * (4 - x)
    group, step = 4, 1024

    loads = [
        pltpu.make_async_copy(key_ref, raw.at[0], load_sem.at[0]),
        pltpu.make_async_copy(value_ref, raw.at[1], load_sem.at[1]),
    ]
    for load in loads:
        load.start()
    barrier = pltpu.get_barrier_semaphore()

    def greet(d, _):
        pl.semaphore_signal(
            barrier, inc=1, device_id={"seq": lax.rem(me + d, owners)}, device_id_type=MESH
        )
        return 0

    lax.fori_loop(1, owners, greet, 0)

    def ahead(offset):
        dz, dx, dc = offset
        return lax.rem(z + dz, 4) * 8 + lax.rem(x + dx, 4) * 2 + lax.rem(core + dc, 2)

    def behind(offset):
        dz, dx, dc = offset
        return lax.rem(z + 4 - dz, 4) * 8 + lax.rem(x + 4 - dx, 4) * 2 + lax.rem(core + dc, 2)

    def outward(k, to):
        return pltpu.make_async_remote_copy(
            src_ref=out_ref.at[to],
            dst_ref=arrived.at[k],
            send_sem=send_sem.at[k],
            recv_sem=recv_sem.at[k],
            device_id={"seq": to},
            device_id_type=MESH,
        )

    def homeward(k, to):
        return pltpu.make_async_remote_copy(
            src_ref=done.at[k],
            dst_ref=ret.at[k],
            send_sem=back_sem.at[k],
            recv_sem=home_sem.at[k],
            device_id={"seq": to},
            device_id_type=MESH,
        )

    def kv_copy(d):
        return pltpu.make_async_remote_copy(
            src_ref=kv_ref,
            dst_ref=kvs.at[2 * d + core],
            send_sem=kv_send.at[d],
            recv_sem=kv_recv.at[d],
            device_id={"seq": lax.rem(me + 2 * d, owners)},
            device_id_type=MESH,
        )

    def kv_spread(o):
        other = lax.rem(x + o, 4)
        return pltpu.make_async_remote_copy(
            src_ref=kvs.at[9],
            dst_ref=kvs.at[2 * (4 + other - x) + 1],
            send_sem=spread_send.at[o],
            recv_sem=kv_recv.at[4 + other - x],
            device_id={"seq": z * 8 + other * 2 + 1},
            device_id_type=MESH,
        )

    def kv_beside():
        return pltpu.make_async_remote_copy(
            src_ref=kv_ref,
            dst_ref=kvs.at[0],
            send_sem=kv_send.at[0],
            recv_sem=kv_recv.at[0],
            device_id={"seq": sibling},
            device_id_type=MESH,
        )

    def kv_forward(d, from_core):
        return pltpu.make_async_remote_copy(
            src_ref=kvs.at[2 * d + from_core],
            dst_ref=kvs.at[2 * d + from_core],
            send_sem=fwd_send.at[d],
            recv_sem=fwd_recv.at[d],
            device_id={"seq": sibling},
            device_id_type=MESH,
        )

    span = 2 * feature
    row = lax.broadcasted_iota(jnp.int32, (span, span), 0)
    col = lax.broadcasted_iota(jnp.int32, (span, span), 1)
    picking = (col == 2 * lax.rem(row, feature) + lax.div(row, feature)).astype(jnp.bfloat16)
    placing = (row == 2 * lax.rem(col, feature) + lax.div(col, feature)).astype(jnp.bfloat16)

    for j in range(new_key_ref.shape[0] // span):
        cut = slice(j * feature, (j + 1) * feature)
        block = new_key_ref[j * span : (j + 1) * span, :]
        both = jnp.dot(picking, block, preferred_element_type=jnp.float32).astype(jnp.bfloat16)
        for h in range(heads):
            kv_ref[0, h, cut, :] = both[h * feature : (h + 1) * feature, :]
        block = new_value_ref[j * span : (j + 1) * span, :]
        both = lax.dot_general(block, placing, TN, preferred_element_type=jnp.float32)
        both = both.astype(jnp.bfloat16)
        for h in range(heads):
            kv_ref[1, h, cut, :] = both[:, h * feature : (h + 1) * feature]

    pl.semaphore_wait(barrier, owners - 1)

    def start_out(i, digits):
        for j, offset in enumerate(offsets_of(digits)):
            k = i * group + j
            if j == 0:

                @pl.when(i > 0)
                def _():
                    outward(k, ahead(offset)).start()

            else:
                outward(k, ahead(offset)).start()
        return next_digits(digits)

    digits = lax.fori_loop(0, EARLY, start_out, first_digits())

    def start_kv(d, _):
        kv_copy(d).start()
        return 0

    lax.fori_loop(1, sent_until, start_kv, 0)

    @pl.when((1 - lower) * core == 1)
    def _():
        kv_copy(4).start()

    @pl.when(core == 0)
    def _():
        kv_beside().start()

    lax.fori_loop(EARLY, owners // group, start_out, digits)
    arrived[0] = out_ref[me]
    loads[0].wait()

    def sort_keys(j, _):
        block = raw[0, pl.ds(pl.multiple_of(j * span, span), span), :]
        both = jnp.dot(picking, block, preferred_element_type=jnp.float32).astype(jnp.bfloat16)
        for h in range(heads):
            keys[h, pl.ds(pl.multiple_of(j * feature, feature), feature), :] = both[
                h * feature : (h + 1) * feature, :
            ]
        return 0

    lax.fori_loop(0, KB // feature, sort_keys, 0, unroll=4)
    loads[1].wait()

    def sort_values(j, _):
        block = raw[1, pl.ds(pl.multiple_of(j * span, span), span), :]
        both = lax.dot_general(block, placing, TN, preferred_element_type=jnp.float32)
        both = both.astype(jnp.bfloat16)
        for h in range(heads):
            values[h, :, pl.ds(pl.multiple_of(j * feature, feature), feature)] = both[
                :, h * feature : (h + 1) * feature
            ]
        return 0

    lax.fori_loop(0, KB // feature, sort_values, 0, unroll=4)

    spreads = lower * core

    def own_attention():
        item = slot_rows // 2
        block_rows = item // 4
        half = kv_ref.shape[2] // 2

        def pass_on(d, _):
            @pl.when(jnp.logical_or(d != 4, spreads == 0))
            def _():
                kv_copy(d).wait_recv()

            kv_forward(d, core).start()
            return 0

        lax.fori_loop(1, place + 1, pass_on, 0)

        def absorb(pairs, first):
            for h in range(heads):
                split = split_queries(q_ref[h])
                key_rows = [ref[0, h] for ref in pairs]
                key_rows = key_rows[0] if len(pairs) == 1 else jnp.concatenate(key_rows, axis=0)
                value_t = jnp.concatenate(
                    [ref[1, h, at : at + half, :] for ref in pairs for at in (0, half)], axis=1
                )
                s = scores_of(key_rows, split)
                if first:
                    key_at = lax.broadcasted_iota(jnp.int32, s.shape, 0)
                    lane = lax.broadcasted_iota(jnp.int32, s.shape, 1)
                    row_at = (lane // item) * block_rows + lax.rem(lane, block_rows)
                    s = jnp.where(key_at <= row_at, s, -1e30)
                best = jnp.max(s, axis=0, keepdims=True)
                if not first:
                    best = jnp.maximum(top_ref[h, 0:1, :], best)
                e = jnp.exp2(s - best)
                part = jnp.sum(e, axis=0, keepdims=True)
                o = jnp.dot(value_t, e.astype(jnp.bfloat16), preferred_element_type=jnp.float32)
                if first:
                    acc_ref[h] = o
                    sum_ref[h, 0:1, :] = part
                else:
                    fade = jnp.exp2(top_ref[h, 0:1, :] - best)
                    acc_ref[h] = acc_ref[h] * fade + o
                    sum_ref[h, 0:1, :] = sum_ref[h, 0:1, :] * fade + part
                top_ref[h, 0:1, :] = best

        absorb([kv_ref], True)

        @pl.when(core == 1)
        def _():
            kv_beside().wait_recv()
            absorb([kvs.at[0]], False)

        def two(d, _):
            kv_forward(d, core).wait_recv()
            absorb([kvs.at[2 * d], kvs.at[2 * d + 1]], False)
            return 0

        lax.fori_loop(1, place + 1, two, 0)
        for h in range(heads):
            total = sum_ref[h, 0:1, :]
            own_ref[h] = (acc_ref[h] / total).T
            lse_ref[h] = jnp.broadcast_to(top_ref[h, 0:1, :] + jnp.log2(total), lse_ref.shape[1:])

    def tile(i, digits):
        first = i * group

        @pl.when(jnp.logical_and(i == SPREAD_AT, spreads == 1))
        def _():
            kv_copy(4).wait_recv()
            for o in range(1, 4):
                kv_spread(o).start()

        @pl.when(i == OWN_AT)
        def _():
            own_attention()

        offsets = offsets_of(digits)
        for j, offset in enumerate(offsets):
            if j == 0:

                @pl.when(i > 0)
                def _():
                    outward(first, sibling).wait_recv()

            else:
                outward(first + j, sibling).wait_recv()
        lses = []
        for h in range(heads):
            rows = jnp.concatenate([arrived[first + j, h] for j in range(group)], axis=0)
            out, lse = attend_tile(
                rows,
                lambda c: keys[h, c * step : (c + 1) * step, :],
                lambda c: values[h, :, c * step : (c + 1) * step],
                KB // step,
            )
            out = out.T.astype(jnp.bfloat16)
            lses.append(lse)
            for j in range(group):
                cut = slice(j * slot_rows, (j + 1) * slot_rows)
                done[first + j, h * slot_rows : (h + 1) * slot_rows, :] = out[cut, :]
        for j, offset in enumerate(offsets):
            cut = slice(j * slot_rows, (j + 1) * slot_rows)
            done[first + j, heads * slot_rows : heads * slot_rows + EXTRA, :] = three_parts(
                [lse[:, cut] for lse in lses]
            )
            if j == 0:

                @pl.when(i > 0)
                def _():
                    homeward(first, behind(offset)).start()

            else:
                homeward(first + j, behind(offset)).start()
        return next_digits(digits)

    lax.fori_loop(0, owners // group, tile, first_digits())
    ret[0] = done[0]

    def finish(k, _):
        homeward(k, sibling).wait_recv()
        outward(k, sibling).wait_send()
        homeward(k, sibling).wait_send()
        return 0

    lax.fori_loop(1, owners, finish, 0)

    def finish_kv(d, _):
        kv_copy(d).wait_send()
        return 0

    lax.fori_loop(1, sent_until, finish_kv, 0)

    @pl.when((1 - lower) * core == 1)
    def _():
        kv_copy(4).wait_send()

    @pl.when(spreads == 1)
    def _():
        for o in range(1, 4):
            kv_spread(o).wait_send()

    @pl.when(core == 0)
    def _():
        kv_beside().wait_send()

    def finish_forward(d, _):
        kv_forward(d, core).wait_send()
        return 0

    lax.fori_loop(1, place + 1, finish_forward, 0)


def merge_kernel(picks_ref, slot_ref, table_ref, own_ref, own_lse_ref, ret, merged_ref):
    heads = own_ref.shape[0]
    feature = own_ref.shape[2]
    blocks, picked = picks_ref.shape[1:]
    item = own_ref.shape[1] // blocks
    block_rows = merged_ref.shape[0] // blocks
    fold = item // block_rows
    me = lax.axis_index("seq")
    z, x, core = lax.div(me, 8), lax.rem(lax.div(me, 2), 4), lax.rem(me, 2)

    def place_of(t):
        dz = lax.rem(lax.div(t, 8) - z + 4, 4)
        dx = lax.rem(lax.rem(lax.div(t, 2), 4) - x + 4, 4)
        return 2 * table_ref[dz, dx] + lax.rem(lax.rem(t, 2) - core + 2, 2)

    for h in range(heads):
        own = own_ref[h]
        lses = [own_lse_ref[h, 0:1, :]]
        for p in range(picked):
            pieces = []
            for b in range(blocks):
                at, c = place_of(picks_ref[h, b, p]), slot_ref[h, b, p]
                extra = ret[at, heads * 2 * item : heads * 2 * item + EXTRA, :]
                lse = jnp.sum(
                    extra.astype(jnp.float32)[3 * h : 3 * h + 3, :], axis=0, keepdims=True
                )
                pieces.append(jnp.where(c == 0, lse[:, 0:item], lse[:, item : 2 * item]))
            lses.append(jnp.concatenate(pieces, axis=1))
        best = functools.reduce(jnp.maximum, lses)
        shares = [jnp.exp2(x - best) for x in lses]
        whole = functools.reduce(jnp.add, shares)
        shares = [x / whole for x in shares]
        fill = [jnp.zeros_like(best)] * (8 - len(shares))
        columns = jnp.concatenate(shares + fill, axis=0).T
        for b in range(blocks):
            cut = slice(b * item, (b + 1) * item)
            mix = own[cut, :] * columns[cut, 0:1]
            for p in range(picked):
                at, c = place_of(picks_ref[h, b, p]), slot_ref[h, b, p]
                got = ret[at, pl.ds(pl.multiple_of((2 * h + c) * item, item), item), :]
                mix = mix + got.astype(jnp.float32) * columns[cut, p + 1 : p + 2]
            mix = mix.astype(jnp.bfloat16)
            for g in range(fold):
                lane = (h * fold + g) * feature
                merged_ref[b * block_rows : (b + 1) * block_rows, lane : lane + feature] = mix[
                    g * block_rows : (g + 1) * block_rows, :
                ]


def merge(picks, slots, own, lse, ret):
    table = [[0] * 4 for _ in range(4)]
    for i, pair in enumerate(CHIPS):
        for j, (dz, dx) in enumerate(pair):
            table[dz][dx] = 2 * i + j
    table = jnp.array(table, jnp.int32)
    return pl.pallas_call(
        merge_kernel,
        out_shape=jax.ShapeDtypeStruct((256, 8 * own.shape[2]), jnp.bfloat16),
        in_specs=[SM, SM, SM, VM, VM, VM],
        out_specs=VM,
        compiler_params=pltpu.CompilerParams(vmem_limit_bytes=BIG),
    )(picks, slots, table, own, lse, ret)


def exchange(outgoing, keys, values, q, new_keys, new_values):
    owners, heads, slot_rows, feature = outgoing.shape
    rows = q.shape[1]
    kv_shape = (2, heads, new_keys.shape[0] // heads, feature)
    back = (owners, heads * slot_rows + EXTRA, feature)
    dma = pltpu.SemaphoreType.DMA
    return pl.pallas_call(
        exchange_kernel,
        out_shape=(
            jax.ShapeDtypeStruct(back, jnp.bfloat16),
            jax.ShapeDtypeStruct((heads, rows, feature), jnp.float32),
            jax.ShapeDtypeStruct((heads, 8, rows), jnp.float32),
        ),
        in_specs=[VM, ANY, ANY, VM, VM, VM],
        out_specs=(VM, VM, VM),
        scratch_shapes=[
            pltpu.VMEM(kv_shape, jnp.bfloat16),
            pltpu.VMEM((2,) + keys.shape, jnp.bfloat16),
            pltpu.VMEM((heads, KB, feature), jnp.bfloat16),
            pltpu.VMEM((heads, feature, KB), jnp.bfloat16),
            pltpu.VMEM(outgoing.shape, jnp.bfloat16),
            pltpu.VMEM(back, jnp.bfloat16),
            pltpu.VMEM((16,) + kv_shape, jnp.bfloat16),
            pltpu.VMEM((heads, feature, rows), jnp.float32),
            pltpu.VMEM((heads, 8, rows), jnp.float32),
            pltpu.VMEM((heads, 8, rows), jnp.float32),
            dma((2,)),
            dma((owners,)),
            dma((owners,)),
            dma((owners,)),
            dma((owners,)),
            dma((8,)),
            dma((8,)),
            dma((8,)),
            dma((8,)),
            dma((4,)),
        ],
        compiler_params=pltpu.CompilerParams(
            collective_id=0, has_side_effects=True, vmem_limit_bytes=BIG
        ),
    )(outgoing, keys, values, q, new_keys, new_values)


def project_kernel(
    m_ref, w_ref, out_ref, w_buf, order, sent1, keep, got1, sent2, mine2, got2,
    load_sem, send1, recv1, send2, recv2,
):
    parts, depth, wide = w_buf.shape
    y = lax.axis_index("kvh")
    beside = y + 1 - 2 * lax.rem(y, 2)
    across = 3 - y
    far = 3 - beside
    rows = m_ref.shape[0] // 4

    loads = [
        pltpu.make_async_copy(w_ref.at[:, n * wide : (n + 1) * wide], w_buf.at[n], load_sem.at[n])
        for n in range(parts)
    ]
    for load in loads:
        load.start()
    barrier = pltpu.get_barrier_semaphore()
    for other in (beside, across):
        pl.semaphore_signal(barrier, inc=1, device_id={"kvh": other}, device_id_type=MESH)
    for kind, blocks in enumerate(((beside, far, across, y), (across, far, beside, y))):
        for i, b in enumerate(blocks):
            order[kind, i * rows : (i + 1) * rows, :] = m_ref[
                pl.ds(pl.multiple_of(b * rows, rows), rows), :
            ]
    pl.semaphore_wait(barrier, 2)

    def first_copy(n):
        return pltpu.make_async_remote_copy(
            src_ref=sent1.at[n],
            dst_ref=got1.at[n],
            send_sem=send1.at[n],
            recv_sem=recv1.at[n],
            device_id={"kvh": beside if n % 2 == 0 else across},
            device_id_type=MESH,
        )

    def second_copy(n):
        return pltpu.make_async_remote_copy(
            src_ref=sent2.at[n],
            dst_ref=got2.at[n],
            send_sem=send2.at[n],
            recv_sem=recv2.at[n],
            device_id={"kvh": across if n % 2 == 0 else beside},
            device_id_type=MESH,
        )

    def forward(n):
        first_copy(n).wait_recv()
        both = got1[n].astype(jnp.float32)
        sent2[n] = (keep[n, 0:rows, :] + both[rows:, :]).astype(jnp.bfloat16)
        mine2[n] = keep[n, rows:, :] + both[0:rows, :]
        second_copy(n).start()

    for n in range(parts):
        loads[n].wait()
        product = jnp.dot(order[n % 2], w_buf[n], preferred_element_type=jnp.float32)
        sent1[n] = product[0 : 2 * rows, :].astype(jnp.bfloat16)
        keep[n] = product[2 * rows :, :]
        first_copy(n).start()
        if n >= LAG:
            forward(n - LAG)
    for n in range(parts - LAG, parts):
        forward(n)
    for n in range(parts):
        second_copy(n).wait_recv()
        out_ref[:, n * wide : (n + 1) * wide] = (
            mine2[n] + got2[n].astype(jnp.float32)
        ).astype(jnp.bfloat16)
    for n in range(parts):
        first_copy(n).wait_send()
        second_copy(n).wait_send()


def project(merged, weight):
    rows, depth = merged.shape
    width = weight.shape[1]
    parts = 16
    wide = width // parts
    quarter = rows // 4
    dma = pltpu.SemaphoreType.DMA
    return pl.pallas_call(
        project_kernel,
        out_shape=jax.ShapeDtypeStruct((quarter, width), jnp.bfloat16),
        in_specs=[VM, ANY],
        out_specs=VM,
        scratch_shapes=[
            pltpu.VMEM((parts, depth, wide), jnp.bfloat16),
            pltpu.VMEM((2, rows, depth), jnp.bfloat16),
            pltpu.VMEM((parts, 2 * quarter, wide), jnp.bfloat16),
            pltpu.VMEM((parts, 2 * quarter, wide), jnp.float32),
            pltpu.VMEM((parts, 2 * quarter, wide), jnp.bfloat16),
            pltpu.VMEM((parts, quarter, wide), jnp.bfloat16),
            pltpu.VMEM((parts, quarter, wide), jnp.float32),
            pltpu.VMEM((parts, quarter, wide), jnp.bfloat16),
            dma((parts,)),
            dma((parts,)),
            dma((parts,)),
            dma((parts,)),
            dma((parts,)),
        ],
        compiler_params=pltpu.CompilerParams(
            collective_id=1, has_side_effects=True, vmem_limit_bytes=BIG
        ),
    )(merged, weight)


def on_device(queries, ctx_keys, ctx_values, new_keys, new_values, picks, out_weight):
    outgoing, slots, q = place(picks, queries.reshape(2048, 128))
    flat = [x.reshape(-1, 128) for x in (ctx_keys, ctx_values, new_keys, new_values)]
    ret, own, lse = exchange(outgoing, flat[0], flat[1], q, flat[2], flat[3])
    merged = merge(picks, slots, own, lse, ret)
    return project(merged, out_weight)


def solution(mesh):
    placed = (
        P("seq", "kvh", None),
        P("seq", "kvh", None),
        P("seq", "kvh", None),
        P("seq", "kvh", None),
        P("seq", "kvh", None),
        P("kvh", "seq", None),
        P("kvh", None),
    )
    return jax.shard_map(
        on_device, mesh=mesh, in_specs=placed, out_specs=P(("seq", "kvh"), None), check_vma=False
    )
```

```python
import functools

import jax
import jax.numpy as jnp
from jax import lax
from jax.experimental import pallas as pl
from jax.experimental.pallas import tpu as pltpu
from jax.sharding import PartitionSpec as P

LOG2E = 1.4426950408889634
NT = (((1,), (1,)), ((), ()))
TN = (((0,), (0,)), ((), ()))
VM = pl.BlockSpec(memory_space=pltpu.VMEM)
SM = pl.BlockSpec(memory_space=pltpu.SMEM)
KB = 4096
BIG = 60 * 2**20
EXTRA = 16
LAG = 3
EARLY = 4
SPREAD_AT = 5
MESH = pl.DeviceIdType.MESH
ANY = pl.BlockSpec(memory_space=pl.ANY)


def split_queries(rows):
    scale = LOG2E * float(rows.shape[-1]) ** -0.5
    scaled = rows.astype(jnp.float32) * scale
    high = scaled.astype(jnp.bfloat16)
    low = (scaled - high.astype(jnp.float32)).astype(jnp.bfloat16)
    return jnp.concatenate([high, low], axis=1)


def scores_of(keys, split):
    return lax.dot_general(
        jnp.concatenate([keys, keys], axis=1), split, NT, preferred_element_type=jnp.float32
    )


def attend_tile(rows, keys_at, values_t_at, chunks):
    split = split_queries(rows)
    top = total = acc = None
    now = scores_of(keys_at(0), split)
    for c in range(chunks):
        later = scores_of(keys_at(c + 1), split) if c + 1 < chunks else None
        best = jnp.max(now, axis=0, keepdims=True)
        best = best if top is None else jnp.maximum(top, best)
        e = jnp.exp2(now - best)
        part = jnp.sum(e, axis=0, keepdims=True)
        out = jnp.dot(values_t_at(c), e.astype(jnp.bfloat16), preferred_element_type=jnp.float32)
        if top is None:
            acc, total = out, part
        else:
            fade = jnp.exp2(top - best)
            acc, total = acc * fade + out, total * fade + part
        top, now = best, later
    return acc / total, top + jnp.log2(total)


def three_parts(rows):
    parts = []
    for row in rows:
        high = row.astype(jnp.bfloat16).astype(jnp.float32)
        rest = row - high
        mid = rest.astype(jnp.bfloat16).astype(jnp.float32)
        parts += [high, mid, rest - mid]
    fill = jnp.zeros((EXTRA - len(parts), rows[0].shape[1]), jnp.float32)
    return jnp.concatenate(parts + [fill], axis=0).astype(jnp.bfloat16)


CHIPS = (
    ((0, 0), (0, 1)), ((1, 0), (0, 3)), ((3, 0), (1, 1)), ((3, 3), (1, 3)),
    ((3, 1), (0, 2)), ((2, 0), (1, 2)), ((2, 1), (3, 2)), ((2, 3), (2, 2)),
)
DIGITS = tuple(
    sum(pair[a][b] * 4**i for i, pair in enumerate(CHIPS)) for a in range(2) for b in range(2)
)


def offsets_of(digits):
    za, xa, zb, xb = [lax.rem(x, 4) for x in digits]
    return ((za, xa, 0), (za, xa, 1), (zb, xb, 0), (zb, xb, 1))


def next_digits(digits):
    return tuple(lax.div(x, 4) for x in digits)


def first_digits():
    return tuple(jnp.int32(x) for x in DIGITS)


def place_kernel(picks_ref, raw_ref, out_ref, slot_ref, q_ref, count_ref):
    heads, blocks, picked = picks_ref.shape
    item = q_ref.shape[1] // blocks
    both = heads * item
    streams = both // 16
    to = lax.broadcasted_iota(jnp.int32, (both, both), 0)
    frm = lax.broadcasted_iota(jnp.int32, (both, both), 1)
    picking = (frm == lax.rem(to, 16) * streams + lax.div(to, 16)).astype(jnp.bfloat16)
    for b in range(blocks):
        rows = jnp.dot(
            picking, raw_ref[b * both : (b + 1) * both, :], preferred_element_type=jnp.float32
        ).astype(jnp.bfloat16)
        for h in range(heads):
            q_ref[h, b * item : (b + 1) * item, :] = rows[h * item : (h + 1) * item, :]
    owners = out_ref.shape[0]
    out_ref[...] = jnp.zeros_like(out_ref)

    def clear(i, _):
        for h in range(heads):
            count_ref[h, i] = 0
        return 0

    lax.fori_loop(0, owners, clear, 0)
    for h in range(heads):

        def one(q, _):
            rows = q_ref[h, pl.ds(pl.multiple_of(q * item, item), item), :]
            for p in range(picked):
                t = picks_ref[h, q, p]
                c = count_ref[h, t]
                count_ref[h, t] = c + 1
                slot_ref[h, q, p] = c
                out_ref[t, h, pl.ds(pl.multiple_of(c * item, item), item), :] = rows
            return 0

        lax.fori_loop(0, blocks, one, 0)


def place(picks, raw):
    heads, blocks, picked = picks.shape
    feature = raw.shape[1]
    rows = raw.shape[0] // heads
    return pl.pallas_call(
        place_kernel,
        out_shape=(
            jax.ShapeDtypeStruct((32, heads, 128, feature), jnp.bfloat16),
            jax.ShapeDtypeStruct(picks.shape, jnp.int32),
            jax.ShapeDtypeStruct((heads, rows, feature), jnp.bfloat16),
        ),
        in_specs=[SM, VM],
        out_specs=(VM, SM, VM),
        scratch_shapes=[pltpu.SMEM((heads, 32), jnp.int32)],
        compiler_params=pltpu.CompilerParams(vmem_limit_bytes=BIG),
    )(picks, raw)


def exchange_kernel(
    out_ref, key_ref, value_ref, q_ref, new_key_ref, new_value_ref, ret, own_ref, lse_ref,
    kv_ref, raw, keys, values, arrived, done, kvs, acc_ref, top_ref, sum_ref,
    load_sem, send_sem, recv_sem, back_sem, home_sem, kv_send, kv_recv, fwd_send, fwd_recv, spread_send,
):
    owners, heads, slot_rows, feature = out_ref.shape
    me = lax.axis_index("seq")
    z, x, core = lax.div(me, 8), lax.rem(lax.div(me, 2), 4), lax.rem(me, 2)
    sibling = me + 1 - 2 * core
    lower = lax.rem(z, 2)
    place = lower * 4 + x
    sent_until = (1 - core) * (8 - place) + core * (4 - x)
    group, step = 4, 1024

    loads = [
        pltpu.make_async_copy(key_ref, raw.at[0], load_sem.at[0]),
        pltpu.make_async_copy(value_ref, raw.at[1], load_sem.at[1]),
    ]
    for load in loads:
        load.start()
    barrier = pltpu.get_barrier_semaphore()

    def greet(d, _):
        pl.semaphore_signal(
            barrier, inc=1, device_id={"seq": lax.rem(me + d, owners)}, device_id_type=MESH
        )
        return 0

    lax.fori_loop(1, owners, greet, 0)

    def ahead(offset):
        dz, dx, dc = offset
        return lax.rem(z + dz, 4) * 8 + lax.rem(x + dx, 4) * 2 + lax.rem(core + dc, 2)

    def behind(offset):
        dz, dx, dc = offset
        return lax.rem(z + 4 - dz, 4) * 8 + lax.rem(x + 4 - dx, 4) * 2 + lax.rem(core + dc, 2)

    def outward(k, to):
        return pltpu.make_async_remote_copy(
            src_ref=out_ref.at[to],
            dst_ref=arrived.at[k],
            send_sem=send_sem.at[k],
            recv_sem=recv_sem.at[k],
            device_id={"seq": to},
            device_id_type=MESH,
        )

    def homeward(k, to):
        return pltpu.make_async_remote_copy(
            src_ref=done.at[k],
            dst_ref=ret.at[k],
            send_sem=back_sem.at[k],
            recv_sem=home_sem.at[k],
            device_id={"seq": to},
            device_id_type=MESH,
        )

    def kv_copy(d):
        return pltpu.make_async_remote_copy(
            src_ref=kv_ref,
            dst_ref=kvs.at[2 * d + core],
            send_sem=kv_send.at[d],
            recv_sem=kv_recv.at[d],
            device_id={"seq": lax.rem(me + 2 * d, owners)},
            device_id_type=MESH,
        )

    def kv_spread(o):
        other = lax.rem(x + o, 4)
        return pltpu.make_async_remote_copy(
            src_ref=kvs.at[9],
            dst_ref=kvs.at[2 * (4 + other - x) + 1],
            send_sem=spread_send.at[o],
            recv_sem=kv_recv.at[4 + other - x],
            device_id={"seq": z * 8 + other * 2 + 1},
            device_id_type=MESH,
        )

    def kv_beside():
        return pltpu.make_async_remote_copy(
            src_ref=kv_ref,
            dst_ref=kvs.at[0],
            send_sem=kv_send.at[0],
            recv_sem=kv_recv.at[0],
            device_id={"seq": sibling},
            device_id_type=MESH,
        )

    def kv_forward(d, from_core):
        return pltpu.make_async_remote_copy(
            src_ref=kvs.at[2 * d + from_core],
            dst_ref=kvs.at[2 * d + from_core],
            send_sem=fwd_send.at[d],
            recv_sem=fwd_recv.at[d],
            device_id={"seq": sibling},
            device_id_type=MESH,
        )

    span = 2 * feature
    row = lax.broadcasted_iota(jnp.int32, (span, span), 0)
    col = lax.broadcasted_iota(jnp.int32, (span, span), 1)
    picking = (col == 2 * lax.rem(row, feature) + lax.div(row, feature)).astype(jnp.bfloat16)
    placing = (row == 2 * lax.rem(col, feature) + lax.div(col, feature)).astype(jnp.bfloat16)

    for j in range(new_key_ref.shape[0] // span):
        cut = slice(j * feature, (j + 1) * feature)
        block = new_key_ref[j * span : (j + 1) * span, :]
        both = jnp.dot(picking, block, preferred_element_type=jnp.float32).astype(jnp.bfloat16)
        for h in range(heads):
            kv_ref[0, h, cut, :] = both[h * feature : (h + 1) * feature, :]
        block = new_value_ref[j * span : (j + 1) * span, :]
        both = lax.dot_general(block, placing, TN, preferred_element_type=jnp.float32)
        both = both.astype(jnp.bfloat16)
        for h in range(heads):
            kv_ref[1, h, cut, :] = both[:, h * feature : (h + 1) * feature]

    pl.semaphore_wait(barrier, owners - 1)

    def start_out(i, digits):
        for j, offset in enumerate(offsets_of(digits)):
            k = i * group + j
            if j == 0:

                @pl.when(i > 0)
                def _():
                    outward(k, ahead(offset)).start()

            else:
                outward(k, ahead(offset)).start()
        return next_digits(digits)

    digits = lax.fori_loop(0, EARLY, start_out, first_digits())

    def start_kv(d, _):
        kv_copy(d).start()
        return 0

    lax.fori_loop(1, sent_until, start_kv, 0)

    @pl.when((1 - lower) * core == 1)
    def _():
        kv_copy(4).start()

    @pl.when(core == 0)
    def _():
        kv_beside().start()

    lax.fori_loop(EARLY, owners // group, start_out, digits)
    arrived[0] = out_ref[me]
    loads[0].wait()

    def sort_keys(j, _):
        block = raw[0, pl.ds(pl.multiple_of(j * span, span), span), :]
        both = jnp.dot(picking, block, preferred_element_type=jnp.float32).astype(jnp.bfloat16)
        for h in range(heads):
            keys[h, pl.ds(pl.multiple_of(j * feature, feature), feature), :] = both[
                h * feature : (h + 1) * feature, :
            ]
        return 0

    lax.fori_loop(0, KB // feature, sort_keys, 0, unroll=4)
    loads[1].wait()

    def sort_values(j, _):
        block = raw[1, pl.ds(pl.multiple_of(j * span, span), span), :]
        both = lax.dot_general(block, placing, TN, preferred_element_type=jnp.float32)
        both = both.astype(jnp.bfloat16)
        for h in range(heads):
            values[h, :, pl.ds(pl.multiple_of(j * feature, feature), feature)] = both[
                :, h * feature : (h + 1) * feature
            ]
        return 0

    lax.fori_loop(0, KB // feature, sort_values, 0, unroll=4)

    spreads = lower * core

    def own_attention():
        item = slot_rows // 2
        block_rows = item // 4
        half = kv_ref.shape[2] // 2

        def pass_on(d, _):
            @pl.when(jnp.logical_or(d != 4, spreads == 0))
            def _():
                kv_copy(d).wait_recv()

            kv_forward(d, core).start()
            return 0

        lax.fori_loop(1, place + 1, pass_on, 0)

        def absorb(pairs, first):
            for h in range(heads):
                split = split_queries(q_ref[h])
                key_rows = [ref[0, h] for ref in pairs]
                key_rows = key_rows[0] if len(pairs) == 1 else jnp.concatenate(key_rows, axis=0)
                value_t = jnp.concatenate(
                    [ref[1, h, at : at + half, :] for ref in pairs for at in (0, half)], axis=1
                )
                s = scores_of(key_rows, split)
                if first:
                    key_at = lax.broadcasted_iota(jnp.int32, s.shape, 0)
                    lane = lax.broadcasted_iota(jnp.int32, s.shape, 1)
                    row_at = (lane // item) * block_rows + lax.rem(lane, block_rows)
                    s = jnp.where(key_at <= row_at, s, -1e30)
                best = jnp.max(s, axis=0, keepdims=True)
                if not first:
                    best = jnp.maximum(top_ref[h, 0:1, :], best)
                e = jnp.exp2(s - best)
                part = jnp.sum(e, axis=0, keepdims=True)
                o = jnp.dot(value_t, e.astype(jnp.bfloat16), preferred_element_type=jnp.float32)
                if first:
                    acc_ref[h] = o
                    sum_ref[h, 0:1, :] = part
                else:
                    fade = jnp.exp2(top_ref[h, 0:1, :] - best)
                    acc_ref[h] = acc_ref[h] * fade + o
                    sum_ref[h, 0:1, :] = sum_ref[h, 0:1, :] * fade + part
                top_ref[h, 0:1, :] = best

        absorb([kv_ref], True)

        @pl.when(core == 1)
        def _():
            kv_beside().wait_recv()
            absorb([kvs.at[0]], False)

        def two(d, _):
            kv_forward(d, core).wait_recv()
            absorb([kvs.at[2 * d], kvs.at[2 * d + 1]], False)
            return 0

        lax.fori_loop(1, place + 1, two, 0)
        for h in range(heads):
            total = sum_ref[h, 0:1, :]
            own_ref[h] = (acc_ref[h] / total).T
            lse_ref[h] = jnp.broadcast_to(top_ref[h, 0:1, :] + jnp.log2(total), lse_ref.shape[1:])

    def tile(i, digits):
        first = i * group

        @pl.when(jnp.logical_and(i == SPREAD_AT, spreads == 1))
        def _():
            kv_copy(4).wait_recv()
            for o in range(1, 4):
                kv_spread(o).start()

        offsets = offsets_of(digits)
        for j, offset in enumerate(offsets):
            if j == 0:

                @pl.when(i > 0)
                def _():
                    outward(first, sibling).wait_recv()

            else:
                outward(first + j, sibling).wait_recv()
        lses = []
        for h in range(heads):
            rows = jnp.concatenate([arrived[first + j, h] for j in range(group)], axis=0)
            out, lse = attend_tile(
                rows,
                lambda c: keys[h, c * step : (c + 1) * step, :],
                lambda c: values[h, :, c * step : (c + 1) * step],
                KB // step,
            )
            out = out.T.astype(jnp.bfloat16)
            lses.append(lse)
            for j in range(group):
                cut = slice(j * slot_rows, (j + 1) * slot_rows)
                done[first + j, h * slot_rows : (h + 1) * slot_rows, :] = out[cut, :]
        for j, offset in enumerate(offsets):
            cut = slice(j * slot_rows, (j + 1) * slot_rows)
            done[first + j, heads * slot_rows : heads * slot_rows + EXTRA, :] = three_parts(
                [lse[:, cut] for lse in lses]
            )
            if j == 0:

                @pl.when(i > 0)
                def _():
                    homeward(first, behind(offset)).start()

            else:
                homeward(first + j, behind(offset)).start()
        return next_digits(digits)

    lax.fori_loop(0, owners // group, tile, first_digits())
    own_attention()
    ret[0] = done[0]

    def finish(k, _):
        homeward(k, sibling).wait_recv()
        outward(k, sibling).wait_send()
        homeward(k, sibling).wait_send()
        return 0

    lax.fori_loop(1, owners, finish, 0)

    def finish_kv(d, _):
        kv_copy(d).wait_send()
        return 0

    lax.fori_loop(1, sent_until, finish_kv, 0)

    @pl.when((1 - lower) * core == 1)
    def _():
        kv_copy(4).wait_send()

    @pl.when(spreads == 1)
    def _():
        for o in range(1, 4):
            kv_spread(o).wait_send()

    @pl.when(core == 0)
    def _():
        kv_beside().wait_send()

    def finish_forward(d, _):
        kv_forward(d, core).wait_send()
        return 0

    lax.fori_loop(1, place + 1, finish_forward, 0)


def merge_kernel(picks_ref, slot_ref, table_ref, own_ref, own_lse_ref, ret, merged_ref):
    heads = own_ref.shape[0]
    feature = own_ref.shape[2]
    blocks, picked = picks_ref.shape[1:]
    item = own_ref.shape[1] // blocks
    block_rows = merged_ref.shape[0] // blocks
    fold = item // block_rows
    me = lax.axis_index("seq")
    z, x, core = lax.div(me, 8), lax.rem(lax.div(me, 2), 4), lax.rem(me, 2)

    def place_of(t):
        dz = lax.rem(lax.div(t, 8) - z + 4, 4)
        dx = lax.rem(lax.rem(lax.div(t, 2), 4) - x + 4, 4)
        return 2 * table_ref[dz, dx] + lax.rem(lax.rem(t, 2) - core + 2, 2)

    for h in range(heads):
        own = own_ref[h]
        lses = [own_lse_ref[h, 0:1, :]]
        for p in range(picked):
            pieces = []
            for b in range(blocks):
                at, c = place_of(picks_ref[h, b, p]), slot_ref[h, b, p]
                extra = ret[at, heads * 2 * item : heads * 2 * item + EXTRA, :]
                lse = jnp.sum(
                    extra.astype(jnp.float32)[3 * h : 3 * h + 3, :], axis=0, keepdims=True
                )
                pieces.append(jnp.where(c == 0, lse[:, 0:item], lse[:, item : 2 * item]))
            lses.append(jnp.concatenate(pieces, axis=1))
        best = functools.reduce(jnp.maximum, lses)
        shares = [jnp.exp2(x - best) for x in lses]
        whole = functools.reduce(jnp.add, shares)
        shares = [x / whole for x in shares]
        fill = [jnp.zeros_like(best)] * (8 - len(shares))
        columns = jnp.concatenate(shares + fill, axis=0).T
        for b in range(blocks):
            cut = slice(b * item, (b + 1) * item)
            mix = own[cut, :] * columns[cut, 0:1]
            for p in range(picked):
                at, c = place_of(picks_ref[h, b, p]), slot_ref[h, b, p]
                got = ret[at, pl.ds(pl.multiple_of((2 * h + c) * item, item), item), :]
                mix = mix + got.astype(jnp.float32) * columns[cut, p + 1 : p + 2]
            mix = mix.astype(jnp.bfloat16)
            for g in range(fold):
                lane = (h * fold + g) * feature
                merged_ref[b * block_rows : (b + 1) * block_rows, lane : lane + feature] = mix[
                    g * block_rows : (g + 1) * block_rows, :
                ]


def merge(picks, slots, own, lse, ret):
    table = [[0] * 4 for _ in range(4)]
    for i, pair in enumerate(CHIPS):
        for j, (dz, dx) in enumerate(pair):
            table[dz][dx] = 2 * i + j
    table = jnp.array(table, jnp.int32)
    return pl.pallas_call(
        merge_kernel,
        out_shape=jax.ShapeDtypeStruct((256, 8 * own.shape[2]), jnp.bfloat16),
        in_specs=[SM, SM, SM, VM, VM, VM],
        out_specs=VM,
        compiler_params=pltpu.CompilerParams(vmem_limit_bytes=BIG),
    )(picks, slots, table, own, lse, ret)


def exchange(outgoing, keys, values, q, new_keys, new_values):
    owners, heads, slot_rows, feature = outgoing.shape
    rows = q.shape[1]
    kv_shape = (2, heads, new_keys.shape[0] // heads, feature)
    back = (owners, heads * slot_rows + EXTRA, feature)
    dma = pltpu.SemaphoreType.DMA
    return pl.pallas_call(
        exchange_kernel,
        out_shape=(
            jax.ShapeDtypeStruct(back, jnp.bfloat16),
            jax.ShapeDtypeStruct((heads, rows, feature), jnp.float32),
            jax.ShapeDtypeStruct((heads, 8, rows), jnp.float32),
        ),
        in_specs=[VM, ANY, ANY, VM, VM, VM],
        out_specs=(VM, VM, VM),
        scratch_shapes=[
            pltpu.VMEM(kv_shape, jnp.bfloat16),
            pltpu.VMEM((2,) + keys.shape, jnp.bfloat16),
            pltpu.VMEM((heads, KB, feature), jnp.bfloat16),
            pltpu.VMEM((heads, feature, KB), jnp.bfloat16),
            pltpu.VMEM(outgoing.shape, jnp.bfloat16),
            pltpu.VMEM(back, jnp.bfloat16),
            pltpu.VMEM((16,) + kv_shape, jnp.bfloat16),
            pltpu.VMEM((heads, feature, rows), jnp.float32),
            pltpu.VMEM((heads, 8, rows), jnp.float32),
            pltpu.VMEM((heads, 8, rows), jnp.float32),
            dma((2,)),
            dma((owners,)),
            dma((owners,)),
            dma((owners,)),
            dma((owners,)),
            dma((8,)),
            dma((8,)),
            dma((8,)),
            dma((8,)),
            dma((4,)),
        ],
        compiler_params=pltpu.CompilerParams(
            collective_id=0, has_side_effects=True, vmem_limit_bytes=BIG
        ),
    )(outgoing, keys, values, q, new_keys, new_values)


def project_kernel(
    m_ref, w_ref, out_ref, w_buf, order, sent1, keep, got1, sent2, mine2, got2,
    load_sem, send1, recv1, send2, recv2,
):
    parts, depth, wide = w_buf.shape
    y = lax.axis_index("kvh")
    beside = y + 1 - 2 * lax.rem(y, 2)
    across = 3 - y
    far = 3 - beside
    rows = m_ref.shape[0] // 4

    loads = [
        pltpu.make_async_copy(w_ref.at[:, n * wide : (n + 1) * wide], w_buf.at[n], load_sem.at[n])
        for n in range(parts)
    ]
    for load in loads:
        load.start()
    barrier = pltpu.get_barrier_semaphore()
    for other in (beside, across):
        pl.semaphore_signal(barrier, inc=1, device_id={"kvh": other}, device_id_type=MESH)
    for kind, blocks in enumerate(((beside, far, across, y), (across, far, beside, y))):
        for i, b in enumerate(blocks):
            order[kind, i * rows : (i + 1) * rows, :] = m_ref[
                pl.ds(pl.multiple_of(b * rows, rows), rows), :
            ]
    pl.semaphore_wait(barrier, 2)

    def first_copy(n):
        return pltpu.make_async_remote_copy(
            src_ref=sent1.at[n],
            dst_ref=got1.at[n],
            send_sem=send1.at[n],
            recv_sem=recv1.at[n],
            device_id={"kvh": beside if n % 2 == 0 else across},
            device_id_type=MESH,
        )

    def second_copy(n):
        return pltpu.make_async_remote_copy(
            src_ref=sent2.at[n],
            dst_ref=got2.at[n],
            send_sem=send2.at[n],
            recv_sem=recv2.at[n],
            device_id={"kvh": across if n % 2 == 0 else beside},
            device_id_type=MESH,
        )

    def forward(n):
        first_copy(n).wait_recv()
        both = got1[n].astype(jnp.float32)
        sent2[n] = (keep[n, 0:rows, :] + both[rows:, :]).astype(jnp.bfloat16)
        mine2[n] = keep[n, rows:, :] + both[0:rows, :]
        second_copy(n).start()

    for n in range(parts):
        loads[n].wait()
        product = jnp.dot(order[n % 2], w_buf[n], preferred_element_type=jnp.float32)
        sent1[n] = product[0 : 2 * rows, :].astype(jnp.bfloat16)
        keep[n] = product[2 * rows :, :]
        first_copy(n).start()
        if n >= LAG:
            forward(n - LAG)
    for n in range(parts - LAG, parts):
        forward(n)
    for n in range(parts):
        second_copy(n).wait_recv()
        out_ref[:, n * wide : (n + 1) * wide] = (
            mine2[n] + got2[n].astype(jnp.float32)
        ).astype(jnp.bfloat16)
    for n in range(parts):
        first_copy(n).wait_send()
        second_copy(n).wait_send()


def project(merged, weight):
    rows, depth = merged.shape
    width = weight.shape[1]
    parts = 16
    wide = width // parts
    quarter = rows // 4
    dma = pltpu.SemaphoreType.DMA
    return pl.pallas_call(
        project_kernel,
        out_shape=jax.ShapeDtypeStruct((quarter, width), jnp.bfloat16),
        in_specs=[VM, ANY],
        out_specs=VM,
        scratch_shapes=[
            pltpu.VMEM((parts, depth, wide), jnp.bfloat16),
            pltpu.VMEM((2, rows, depth), jnp.bfloat16),
            pltpu.VMEM((parts, 2 * quarter, wide), jnp.bfloat16),
            pltpu.VMEM((parts, 2 * quarter, wide), jnp.float32),
            pltpu.VMEM((parts, 2 * quarter, wide), jnp.bfloat16),
            pltpu.VMEM((parts, quarter, wide), jnp.bfloat16),
            pltpu.VMEM((parts, quarter, wide), jnp.float32),
            pltpu.VMEM((parts, quarter, wide), jnp.bfloat16),
            dma((parts,)),
            dma((parts,)),
            dma((parts,)),
            dma((parts,)),
            dma((parts,)),
        ],
        compiler_params=pltpu.CompilerParams(
            collective_id=1, has_side_effects=True, vmem_limit_bytes=BIG
        ),
    )(merged, weight)


def on_device(queries, ctx_keys, ctx_values, new_keys, new_values, picks, out_weight):
    outgoing, slots, q = place(picks, queries.reshape(2048, 128))
    flat = [x.reshape(-1, 128) for x in (ctx_keys, ctx_values, new_keys, new_values)]
    ret, own, lse = exchange(outgoing, flat[0], flat[1], q, flat[2], flat[3])
    merged = merge(picks, slots, own, lse, ret)
    return project(merged, out_weight)


def solution(mesh):
    placed = (
        P("seq", "kvh", None),
        P("seq", "kvh", None),
        P("seq", "kvh", None),
        P("seq", "kvh", None),
        P("seq", "kvh", None),
        P("kvh", "seq", None),
        P("kvh", None),
    )
    return jax.shard_map(
        on_device, mesh=mesh, in_specs=placed, out_specs=P(("seq", "kvh"), None), check_vma=False
    )
```
